32 devices in a mesh: seq: 8 (over y, x, core), head: 4 (over z).
Axes of the slice: x: 2, y: 2, z: 4, core: 2. Of those that a mesh axis runs over, the one named last changes fastest.
Arguments:
- tokens: bfloat16 [8192, 512], P(('seq', 'head')), may hold values from -6 to 6
- w_proj: bfloat16 [512, 2048], replicated, may hold values from -0.25 to 0.25
- w_out: bfloat16 [512, 512], replicated, may hold values from -0.25 to 0.25
- tile_user: int32 [64], replicated, may hold values from 0 to 15, never falling along the last dimension, each value on 1 to 40 neighbouring positions
Outputs:
- mixed: bfloat16 [8192, 512], P(('seq', 'head'))
The draws below stay inside these ranges and needn't reach their ends.
Inputs may be any that keep to these rules, and one draw needn't show every extreme that they name: `tile_user`: tile users never fall along the tiles; each user covers 1 to 40 tiles, one exactly 40; every number of 0 to 15 occurs.
All inputs are finite; a program needn't handle non-finite values.
Results may differ from the reference program's by a relative error of at most 0.0052.
Values may be sent and summed in bfloat16 or wider, within the bound.
No kernel may reach another device: no remote copies, remote signals or barrier semaphores. Data moves between devices by JAX's collectives and lax.ppermute only.
A program may use at most 128 MiB of HBM per device.

```python
import math
import jax
import jax.numpy as jnp
import numpy as np
from jax import lax

D = 512
H = 8
DH = 64
TILE = 128
TOKENS = 8192
TILES = 64
USERS = 16
MOST_TILES = 40


def draw_w_proj(key, part):
    columns = H * DH
    pieces = jax.random.split(jax.random.fold_in(key, 5309), 6)
    fluctuation = jax.random.normal(pieces[0], (D, 4 * columns), jnp.float32) / math.sqrt(D)
    strength = 1.4
    toward_query = jax.random.normal(pieces[1], (D, H, 1), jnp.float32) / math.sqrt(D)
    toward_key = jax.random.normal(pieces[2], (D, H, 1), jnp.float32) / math.sqrt(D)
    query_spread = jax.random.uniform(pieces[3], (1, H, DH), jnp.float32, 0.5, 1.5)
    key_spread = jax.random.uniform(pieces[4], (1, H, DH), jnp.float32, 0.5, 1.5)
    value_spread = jax.random.normal(pieces[5], (1, H, DH), jnp.float32)
    blank_cols = jnp.zeros((D, columns), jnp.float32)
    value_part = (toward_key * value_spread).reshape(D, columns)
    query_part = strength * (toward_query * query_spread).reshape(D, columns)
    key_part = strength * (toward_key * key_spread).reshape(D, columns)
    shared = jnp.concatenate([blank_cols, value_part, query_part, key_part], axis=1)
    return jnp.clip(fluctuation + shared, -0.25, 0.25).astype(jnp.bfloat16)


def level_of(own_key, dims, cuts, least, top_value):
    factor_of = 1.0
    for position, parts in cuts:
        steps = jax.random.uniform(jax.random.fold_in(jax.random.fold_in(own_key, 6), position), (parts,), jnp.float32, least / len(cuts), top_value / len(cuts))
        factor_of = factor_of * jnp.repeat(jnp.exp(steps), dims[position] // parts).reshape((-1,) + (1,) * (len(dims) - 1 - position))
    return factor_of


def profile(number_of, total, bound, lean):
    portions = [(1 << 20) // math.isqrt(standing ** lean) + 1 for standing in range(2, number_of + 1)]
    spare, holding = total - bound - (number_of - 1), [1] * (number_of - 1)
    while spare > 0:
        movable = [i for i in range(number_of - 1) if holding[i] < bound]
        whole, budget = sum([portions[i] for i in movable]), spare
        for i in movable:
            more = min(bound - holding[i], max(1, budget * portions[i] // whole), spare)
            holding[i] = holding[i] + more
            spare = spare - more
    return np.array([bound] + holding)


def uneven_parts(rng, amount, total, limit, slope):
    if amount == 2:
        one = jax.random.randint(rng, (), max(1, total - limit), min(limit, total - 1) + 1)
        return jnp.stack([one, total - one])
    sizes = jnp.asarray(profile(amount, total, limit, slope), jnp.int32)
    couples = (amount - 1) // 2
    donor, receiver = sizes[1:1 + 2 * couples:2], sizes[2:2 + 2 * couples:2]
    margin = jnp.minimum(donor - 1, limit - receiver)
    moved = jax.random.randint(jax.random.fold_in(rng, 1), (couples,), 0, 1 << 20) % (margin + 1)
    sizes = sizes.at[1:1 + 2 * couples:2].set(donor - moved).at[2:2 + 2 * couples:2].set(receiver + moved)
    return sizes[jax.random.permutation(jax.random.fold_in(rng, 2), amount)]


def gaussian(key, dims, scale, most, shards=(), kind=jnp.bfloat16):
    result = jax.random.normal(key, dims, jnp.float32) * scale
    if len(shards) > 0:
        result = level_of(key, dims, shards, -0.22, 0.18) * result
    return jnp.clip(result, min=-most, max=most).astype(kind)


def setup_inputs(seed: int = 0) -> dict:
    key_of = jax.random.split(jax.random.key(seed), 5)
    return {
        "tokens": gaussian(key_of[0], (TOKENS, D), 1.0, 6.0, ((0, 32),)),
        "w_proj": draw_w_proj(jax.random.fold_in(key_of[4], 71), 0),
        "w_out": gaussian(key_of[2], (H * DH, D), (H * DH) ** -0.5, 0.25),
        "tile_user": jnp.searchsorted(jnp.cumsum(uneven_parts(key_of[3], USERS, TILES, MOST_TILES, 2)), jnp.arange(TILES), side="right").astype(jnp.int32),
    }


epsilon = 1e-05

def layer_norm(values):
    center = values - lax.optimization_barrier(jnp.mean(values, axis=-1, keepdims=True))
    spread = lax.optimization_barrier(jnp.mean(center * center, axis=-1, keepdims=True))
    return center * lax.rsqrt(spread + epsilon)

def reference(tokens, w_proj, w_out, tile_user):
    columns = H * DH
    inputs = tokens.astype(jnp.float32)
    normed = layer_norm(inputs).astype(jnp.bfloat16)
    projected = jax.nn.silu(jnp.dot(normed, w_proj, preferred_element_type=jnp.float32)).astype(jnp.bfloat16)
    gating = projected[:, :columns]
    values = projected[:, columns:2 * columns]
    queries = projected[:, 2 * columns:3 * columns]
    key_rows = projected[:, 3 * columns:]
    row_user = jnp.repeat(tile_user, TILE)
    tile_length = lax.optimization_barrier(jnp.sum((tile_user[:, None] == tile_user[None, :]).astype(jnp.float32), axis=1)) * TILE
    row_length = jnp.repeat(tile_length, TILE)
    block_rows = math.gcd(TOKENS, 512)
    window_rows = min(TOKENS, MOST_TILES * TILE + block_rows)
    score_scale = DH ** (-0.5)

    def one_block(block_index):
        begin_row = (block_index * block_rows).astype(jnp.int32)
        first_key = jnp.clip(begin_row + block_rows - window_rows, 0, TOKENS - window_rows).astype(jnp.int32)
        query_block = lax.dynamic_slice_in_dim(queries, begin_row, block_rows, 0).reshape(block_rows, H, DH).astype(jnp.float32)
        key_block = lax.dynamic_slice_in_dim(key_rows, first_key, window_rows, 0).reshape(window_rows, H, DH).astype(jnp.float32)
        value_block = lax.dynamic_slice_in_dim(values, first_key, window_rows, 0).reshape(window_rows, H, DH).astype(jnp.float32)
        query_pos = begin_row + jnp.arange(block_rows, dtype=jnp.int32)
        key_pos = first_key + jnp.arange(window_rows, dtype=jnp.int32)
        query_user = lax.dynamic_slice_in_dim(row_user, begin_row, block_rows, 0)
        key_user = lax.dynamic_slice_in_dim(row_user, first_key, window_rows, 0)
        query_length = lax.dynamic_slice_in_dim(row_length, begin_row, block_rows, 0)
        allowed = (query_user[:, None] == key_user[None, :]) & (key_pos[None, :] <= query_pos[:, None])
        scores = jnp.einsum('qhd,khd->hqk', query_block, key_block) * score_scale
        weights = (jnp.where(allowed[None], jax.nn.silu(scores), 0.0) / query_length[None, :, None]).astype(jnp.bfloat16)
        weights = lax.optimization_barrier(weights).astype(jnp.float32)
        return jnp.einsum('hqk,khd->qhd', weights, value_block).reshape(block_rows, columns)
    attention = lax.map(one_block, jnp.arange(TOKENS // block_rows, dtype=jnp.int32)).reshape(TOKENS, columns)
    gated = (layer_norm(attention) * gating.astype(jnp.float32)).astype(jnp.bfloat16)
    return (inputs + jnp.dot(gated, w_out, preferred_element_type=jnp.float32)).astype(jnp.bfloat16)
```

```python
import functools

import jax
import jax.numpy as jnp
from jax import lax
from jax.experimental import pallas as pl
from jax.experimental.pallas import tpu as pltpu
from jax.sharding import PartitionSpec as P

H = 8
DH = 64
TILE = 128
LANES = 2 * DH

epsilon = 1e-05

f32 = jnp.float32
bf16 = jnp.bfloat16


def layer_norm(values):
    center = values - jnp.mean(values, axis=-1, keepdims=True)
    spread = jnp.mean(center * center, axis=-1, keepdims=True)
    return center * lax.rsqrt(spread + epsilon)


def silu(values):
    half = values * 0.5
    return half + half * jnp.tanh(half)


def swap_halves(values):
    return pltpu.roll(values, DH, 1)


def low_lanes(rows):
    return lax.broadcasted_iota(jnp.int32, (rows, LANES), 1) < DH


def project_keys(me_ref, tokens_ref, value_weights, key_weights, *refs):
    outs, held = refs[:-1], refs[-1]
    rows = tokens_ref.shape[0]
    normed = layer_norm(tokens_ref[...].astype(f32)).astype(bf16)
    low = low_lanes(rows)
    for pair in range(H // 2):
        at = slice(pair * LANES, (pair + 1) * LANES)
        values = silu(jnp.dot(normed, value_weights[:, at], preferred_element_type=f32))
        keys = silu(jnp.dot(normed, key_weights[:, at], preferred_element_type=f32))
        held[2 * pair] = jnp.where(low, keys, swap_halves(values)).astype(bf16)
        held[2 * pair + 1] = jnp.where(low, swap_halves(keys), values).astype(bf16)
    for k, out in enumerate(outs):
        out[...] = held[jnp.bitwise_xor(me_ref[0], k)]


def project_queries(me_ref, tokens_ref, query_weights, gating_weights, *refs):
    outs, gating, held = refs[:-2], refs[-2], refs[-1]
    rows = tokens_ref.shape[0]
    half = rows // 2
    normed = layer_norm(tokens_ref[...].astype(f32)).astype(bf16)
    low = low_lanes(half)
    scale = 0.5 * DH ** (-0.5)
    for pair in range(H // 2):
        at = slice(pair * LANES, (pair + 1) * LANES)
        queries = silu(jnp.dot(normed, query_weights[:, at], preferred_element_type=f32)) * scale
        upper, lower = queries[:half], queries[half:]
        held[2 * pair] = jnp.where(low, upper, swap_halves(lower)).astype(bf16)
        held[2 * pair + 1] = jnp.where(low, swap_halves(upper), lower).astype(bf16)
        gating[:, at] = silu(
            jnp.dot(normed, gating_weights[:, at], preferred_element_type=f32)
        ).astype(bf16)
    for k, out in enumerate(outs):
        out[...] = held[jnp.bitwise_xor(me_ref[0], k)]


def attend(start_ref, inverse_ref, block_ref, slot_ref, queries_ref, *refs):
    parts, out_ref, held, sems = refs[:-3], refs[-3], refs[-2], refs[-1]
    step = pl.program_id(0)
    rows = held.shape[1]
    half = rows // 2
    tiles = rows // TILE

    @pl.when(step == 0)
    def _():
        copies, at = [], 0
        for i, part in enumerate(parts):
            copies.append(
                pltpu.make_async_copy(part, held.at[pl.ds(at, part.shape[0])], sems.at[i])
            )
            at += part.shape[0]
        for copy in copies:
            copy.start()
        for copy in copies:
            copy.wait()

    block = block_ref[step]
    first_tile = block * tiles
    last_tile = first_tile + tiles - 1
    start_low, start_high = start_ref[first_tile], start_ref[last_tile]
    low = low_lanes(half)
    packed = queries_ref[0].astype(f32)
    queries = jnp.concatenate(
        [jnp.where(low, packed, 0.0), jnp.where(low, swap_halves(packed), 0.0)], axis=0
    ).astype(bf16)

    def scores_of(key_rows):
        half_score = lax.dot_general(
            queries, key_rows, (((1,), (1,)), ((), ())), preferred_element_type=f32
        )
        return half_score + half_score * jnp.tanh(half_score)

    def plain(key_block, total):
        key_rows = held[slot_ref[key_block]]
        weights = scores_of(key_rows).astype(bf16)
        return total + jnp.dot(weights, key_rows, preferred_element_type=f32)

    def masked(key_block, total):
        key_rows = held[slot_ref[key_block]]
        row = lax.broadcasted_iota(jnp.int32, (rows, 1), 0)
        row_start = jnp.where(row < half, start_low, start_high) * TILE - key_block * rows
        row_last = row + (block - key_block) * rows
        column = lax.broadcasted_iota(jnp.int32, (rows, rows), 1)
        allowed = (column >= row_start) & (column <= row_last)
        weights = jnp.where(allowed, scores_of(key_rows), 0.0).astype(bf16)
        return total + jnp.dot(weights, key_rows, preferred_element_type=f32)

    first = start_low // tiles
    whole = jnp.minimum((start_high + tiles - 1) // tiles, block)
    total = jnp.zeros((rows, LANES), f32)
    total = lax.fori_loop(first, whole, masked, total)
    total = lax.fori_loop(whole, block, plain, total)
    total = masked(block, total)
    upper = total[:half] * inverse_ref[first_tile]
    lower = total[half:] * inverse_ref[last_tile]
    out_ref[0] = jnp.where(low, swap_halves(upper), lower).astype(bf16)


def finish(me_ref, tokens_ref, attention_ref, gating_ref, weights_ref, out_ref):
    rows = tokens_ref.shape[0]
    half = rows // 2
    low = low_lanes(half)
    uppers, lowers = [], []
    for pair in range(H // 2):
        one = attention_ref[jnp.bitwise_xor(me_ref[0], 2 * pair)].astype(f32)
        two = attention_ref[jnp.bitwise_xor(me_ref[0], 2 * pair + 1)].astype(f32)
        uppers.append(jnp.where(low, one, swap_halves(two)))
        lowers.append(jnp.where(low, swap_halves(one), two))
    attention = jnp.concatenate(
        [jnp.concatenate(uppers, axis=1), jnp.concatenate(lowers, axis=1)], axis=0
    )
    gated = (layer_norm(attention) * gating_ref[...].astype(f32)).astype(bf16)
    mixed = tokens_ref[...].astype(f32) + jnp.dot(
        gated, weights_ref[...], preferred_element_type=f32
    )
    out_ref[...] = mixed.astype(bf16)


VMEM = pl.BlockSpec(memory_space=pltpu.VMEM)
SMEM = pl.BlockSpec(memory_space=pltpu.SMEM)
ANY = pl.BlockSpec(memory_space=pl.ANY)


def columns_of(width, block):
    return pl.BlockSpec((width, H * DH), lambda i: (0, block))


def per_device(seq_size, head_size, tokens, w_proj, w_out, tile_user):
    rows, width = tokens.shape
    half = rows // 2
    tiles = rows // TILE
    blocks = seq_size * head_size
    seq, head = lax.axis_index("seq"), lax.axis_index("head")
    fold = H // head_size
    share = fold
    groups = seq_size // (fold * share)
    group, part, core = seq // (fold * share), (seq // share) % fold, seq % share
    me = part * head_size + head
    me_array = me.reshape(1).astype(jnp.int32)

    def partner(array, k):
        if k == 0:
            return array
        pairs = []
        for s in range(seq_size):
            for h in range(head_size):
                g, p, c = s // (fold * share), (s // share) % fold, s % share
                other = (p * head_size + h) ^ k
                t = (g * fold + other // head_size) * share + c
                pairs.append((s * head_size + h, t * head_size + other % head_size))
        return lax.ppermute(array, ("seq", "head"), pairs)

    def seq_flip(array, bit):
        return lax.ppermute(array, "seq", [(s, s ^ bit) for s in range(seq_size)])

    keys_sent = pl.pallas_call(
        project_keys,
        out_shape=[jax.ShapeDtypeStruct((rows, LANES), bf16)] * H,
        grid=(1,),
        in_specs=[SMEM, VMEM, columns_of(width, 1), columns_of(width, 3)],
        out_specs=[VMEM] * H,
        scratch_shapes=[pltpu.VMEM((H, rows, LANES), bf16)],
        name="project_keys",
    )(me_array, tokens, w_proj, w_proj)
    queries_sent = pl.pallas_call(
        project_queries,
        out_shape=[jax.ShapeDtypeStruct((half, LANES), bf16)] * H
        + [jax.ShapeDtypeStruct((rows, H * DH), bf16)],
        grid=(1,),
        in_specs=[SMEM, VMEM, columns_of(width, 2), columns_of(width, 0)],
        out_specs=[VMEM] * (H + 1),
        scratch_shapes=[pltpu.VMEM((H, half, LANES), bf16)],
        name="project_queries",
    )(me_array, tokens, w_proj, w_proj)
    gating = queries_sent[-1]

    arrived = [partner(keys_sent[k], k) for k in range(H)]
    queries = jnp.stack([partner(queries_sent[k], k) for k in range(H)])
    index = jnp.arange(blocks, dtype=jnp.int32)
    block_head, block_seq = index % head_size, index // head_size
    block_core = block_seq % share
    block_me = (block_seq // share % fold) * head_size + block_head
    block_group = block_seq // (share * fold)
    if groups == 2 and share == 2:
        parts = []
        for lot in (jnp.stack(arrived[: H // 2]), jnp.stack(arrived[H // 2 :])):
            far = seq_flip(lot, fold * share)
            parts.append((lot, far, seq_flip(lot, 1), seq_flip(far, 1)))
        parts = [array for lot in parts for array in lot]
        from_me = jnp.bitwise_xor(block_me, me)
        slot = (
            (from_me // (H // 2)) * (2 * H)
            + jnp.bitwise_xor(block_core, core) * H
            + jnp.bitwise_xor(block_group, group) * (H // 2)
            + from_me % (H // 2)
        )
    else:
        everything = lax.all_gather(jnp.stack(arrived), "seq", axis=0, tiled=True)
        parts = [everything]
        slot = block_seq * H + jnp.bitwise_xor(block_me, me)
    asked = jnp.arange(H, dtype=jnp.int32) ^ me
    query_block = (
        (group * fold + asked // head_size) * share + core
    ) * head_size + asked % head_size
    start = jnp.sum((tile_user[None, :] < tile_user[:, None]).astype(jnp.int32), axis=1)
    length = jnp.sum((tile_user[None, :] == tile_user[:, None]).astype(f32), axis=1) * TILE

    held_blocks = sum(array.shape[0] for array in parts)
    attention = pl.pallas_call(
        attend,
        grid_spec=pltpu.PrefetchScalarGridSpec(
            num_scalar_prefetch=4,
            grid=(H,),
            in_specs=[pl.BlockSpec((1, half, LANES), lambda i, *_: (i, 0, 0))]
            + [ANY] * len(parts),
            out_specs=pl.BlockSpec((1, half, LANES), lambda i, *_: (i, 0, 0)),
            scratch_shapes=[
                pltpu.VMEM((held_blocks, rows, LANES), bf16),
                pltpu.SemaphoreType.DMA((len(parts),)),
            ],
        ),
        out_shape=jax.ShapeDtypeStruct((H, half, LANES), bf16),
        compiler_params=pltpu.CompilerParams(vmem_limit_bytes=48 << 20),
        name="attend",
    )(start, 1.0 / length, query_block, slot, queries, *parts)
    returned = jnp.stack([partner(attention[k], k) for k in range(H)])
    return pl.pallas_call(
        finish,
        out_shape=jax.ShapeDtypeStruct((rows, width), bf16),
        in_specs=[SMEM, VMEM, VMEM, VMEM, VMEM],
        out_specs=VMEM,
        name="finish",
    )(me_array, tokens, returned, gating, w_out)


def solution(mesh):
    placed = (P(("seq", "head"), None), P(), P(), P())
    return jax.shard_map(
        functools.partial(per_device, mesh.shape["seq"], mesh.shape["head"]),
        mesh=mesh,
        in_specs=placed,
        out_specs=P(("seq", "head"), None),
        check_vma=False,
    )
```

```python
import functools

import jax
import jax.numpy as jnp
from jax import lax
from jax.experimental import pallas as pl
from jax.experimental.pallas import tpu as pltpu
from jax.sharding import PartitionSpec as P

H = 8
DH = 64
TILE = 128
LANES = 2 * DH
TEAM = H // 2

epsilon = 1e-05

f32 = jnp.float32
bf16 = jnp.bfloat16


def layer_norm(values):
    center = values - jnp.mean(values, axis=-1, keepdims=True)
    spread = jnp.mean(center * center, axis=-1, keepdims=True)
    return center * lax.rsqrt(spread + epsilon)


def silu(values):
    half = values * 0.5
    return half + half * jnp.tanh(half)


def swap_halves(values):
    return pltpu.roll(values, DH, 1)


def low_lanes(rows):
    return lax.broadcasted_iota(jnp.int32, (rows, LANES), 1) < DH


def project_keys(me_ref, tokens_ref, value_weights, key_weights, *refs):
    outs, held = refs[:-1], refs[-1]
    rows = tokens_ref.shape[0]
    normed = layer_norm(tokens_ref[...].astype(f32)).astype(bf16)
    low = low_lanes(rows)
    for pair in range(H // 2):
        at = slice(pair * LANES, (pair + 1) * LANES)
        values = silu(jnp.dot(normed, value_weights[:, at], preferred_element_type=f32))
        keys = silu(jnp.dot(normed, key_weights[:, at], preferred_element_type=f32))
        held[2 * pair] = jnp.where(low, keys, swap_halves(values)).astype(bf16)
        held[2 * pair + 1] = jnp.where(low, swap_halves(keys), values).astype(bf16)
    for k, out in enumerate(outs):
        out[...] = held[jnp.bitwise_xor(me_ref[0], k)]


def project_queries(me_ref, tokens_ref, query_weights, gating_weights, *refs):
    outs, gating, held = refs[:-2], refs[-2], refs[-1]
    rows = tokens_ref.shape[0]
    half = rows // 2
    normed = layer_norm(tokens_ref[...].astype(f32)).astype(bf16)
    low = low_lanes(half)
    scale = 0.5 * DH ** (-0.5)
    for pair in range(H // 2):
        at = slice(pair * LANES, (pair + 1) * LANES)
        queries = silu(jnp.dot(normed, query_weights[:, at], preferred_element_type=f32)) * scale
        upper, lower = queries[:half], queries[half:]
        held[2 * pair] = jnp.where(low, upper, swap_halves(lower)).astype(bf16)
        held[2 * pair + 1] = jnp.where(low, swap_halves(upper), lower).astype(bf16)
        gating[:, at] = silu(
            jnp.dot(normed, gating_weights[:, at], preferred_element_type=f32)
        ).astype(bf16)
    for k, out in enumerate(outs):
        out[...] = held[jnp.bitwise_xor(me_ref[0], k)]


def attend(
    opens, closes, reach_ref, start_ref, inverse_ref, block_ref, slot_ref, queries_ref, *refs
):
    step = pl.program_id(0)
    held, total, queries, sems = refs[-4:]
    out_ref = refs[-5]
    parts = refs[: -5 if opens else -6]
    rows = held.shape[1]
    half = rows // 2
    tiles = rows // TILE

    @pl.when(step == 0)
    def _():
        copies, at = [], 0
        for i, part in enumerate(parts):
            copies.append(
                pltpu.make_async_copy(part, held.at[pl.ds(at, part.shape[0])], sems.at[i])
            )
            at += part.shape[0]
        for copy in copies:
            copy.start()
        for copy in copies:
            copy.wait()

    low = low_lanes(half)
    blocks = [block_ref[reach_ref[2] + step * TEAM + i] for i in range(TEAM)]
    for i in range(TEAM):
        packed = queries_ref[i].astype(f32)
        queries[i * rows : i * rows + half] = jnp.where(low, packed, 0.0).astype(bf16)
        queries[i * rows + half : (i + 1) * rows] = jnp.where(
            low, swap_halves(packed), 0.0
        ).astype(bf16)
    starts = [start_ref[block * tiles + j] for block in blocks for j in range(tiles)]
    least, low_start, high_start = blocks[0], starts[0], starts[0]
    for block in blocks[1:]:
        least = jnp.minimum(least, block)
    for start in starts[1:]:
        low_start = jnp.minimum(low_start, start)
        high_start = jnp.maximum(high_start, start)
    total[...] = jnp.zeros_like(total) if opens else refs[-6][...]

    def add(key_block, count, masked):
        key_rows = [held[slot_ref[key_block + i]] for i in range(count)]
        key_rows = key_rows[0] if count == 1 else jnp.concatenate(key_rows, axis=0)
        if masked:
            column = lax.broadcasted_iota(jnp.int32, (TILE, count * rows), 1)
            ahead = column - lax.broadcasted_iota(jnp.int32, (TILE, count * rows), 0)
        for i in range(TEAM):
            at = slice(i * rows, (i + 1) * rows)
            score = lax.dot_general(
                queries[at], key_rows, (((1,), (1,)), ((), ())), preferred_element_type=f32
            )
            weights = score + score * jnp.tanh(score)
            if masked:
                pieces = []
                for j in range(tiles):
                    from_start = starts[i * tiles + j] * TILE - key_block * rows
                    to_row = (blocks[i] - key_block) * rows + j * TILE
                    allowed = (column >= from_start) & (ahead <= to_row)
                    pieces.append(jnp.where(allowed, weights[j * TILE : (j + 1) * TILE], 0.0))
                weights = jnp.concatenate(pieces, axis=0)
            total[at] += jnp.dot(weights.astype(bf16), key_rows, preferred_element_type=f32)

    def loop(begin, end, count, masked):
        def body(index, carry):
            add(begin + index * count, count, masked)
            return carry

        lax.fori_loop(0, jnp.maximum(end - begin, 0) // count, body, 0)

    reach_low, reach_high = reach_ref[0], jnp.minimum(reach_ref[1], least)
    first = jnp.maximum(low_start // tiles, reach_low)
    whole = jnp.maximum(first, jnp.minimum((high_start + tiles - 1) // tiles, reach_high))
    even = jnp.maximum(whole, jnp.minimum((whole + TEAM - 1) // TEAM * TEAM, reach_high))
    loop(first, whole, 1, True)
    loop(whole, even, 1, False)
    loop(even, reach_high, TEAM, False)

    @pl.when(least < reach_ref[1])
    def _():
        add(least, TEAM, True)

    if not closes:
        out_ref[...] = total[...]
        return
    for i in range(TEAM):
        at = i * rows
        upper = total[at : at + half] * inverse_ref[blocks[i] * tiles]
        lower = total[at + half : at + rows] * inverse_ref[blocks[i] * tiles + tiles - 1]
        out_ref[i] = jnp.where(low, swap_halves(upper), lower).astype(bf16)


def attend_call(tables, reach, queries, parts, before=None, closes=True):
    half, rows = queries.shape[1], 2 * queries.shape[1]
    steps = queries.shape[0] // TEAM
    held_blocks = sum(array.shape[0] for array in parts)
    totals = pl.BlockSpec((TEAM * rows, LANES), lambda i, *_: (i, 0))
    packed = pl.BlockSpec((TEAM, half, LANES), lambda i, *_: (i, 0, 0))
    extra = [] if before is None else [before]
    return pl.pallas_call(
        functools.partial(attend, before is None, closes),
        grid_spec=pltpu.PrefetchScalarGridSpec(
            num_scalar_prefetch=5,
            grid=(steps,),
            in_specs=[packed] + [ANY] * len(parts) + [totals] * len(extra),
            out_specs=packed if closes else totals,
            scratch_shapes=[
                pltpu.VMEM((held_blocks, rows, LANES), bf16),
                pltpu.VMEM((TEAM * rows, LANES), f32),
                pltpu.VMEM((TEAM * rows, LANES), bf16),
                pltpu.SemaphoreType.DMA((len(parts),)),
            ],
        ),
        out_shape=jax.ShapeDtypeStruct(queries.shape, bf16)
        if closes
        else jax.ShapeDtypeStruct((steps * TEAM * rows, LANES), f32),
        compiler_params=pltpu.CompilerParams(vmem_limit_bytes=40 << 20),
        cost_estimate=pl.CostEstimate(
            flops=steps * 2_000_000_000, bytes_accessed=4_000_000, transcendentals=4_000_000
        ),
        name="attend",
    )(reach, *tables, queries, *parts, *extra)


def finish(me_ref, tokens_ref, attention_ref, gating_ref, weights_ref, out_ref):
    rows = tokens_ref.shape[0]
    half = rows // 2
    low = low_lanes(half)
    uppers, lowers = [], []
    for pair in range(H // 2):
        one = attention_ref[jnp.bitwise_xor(me_ref[0], 2 * pair)].astype(f32)
        two = attention_ref[jnp.bitwise_xor(me_ref[0], 2 * pair + 1)].astype(f32)
        uppers.append(jnp.where(low, one, swap_halves(two)))
        lowers.append(jnp.where(low, swap_halves(one), two))
    attention = jnp.concatenate(
        [jnp.concatenate(uppers, axis=1), jnp.concatenate(lowers, axis=1)], axis=0
    )
    gated = (layer_norm(attention) * gating_ref[...].astype(f32)).astype(bf16)
    mixed = tokens_ref[...].astype(f32) + jnp.dot(
        gated, weights_ref[...], preferred_element_type=f32
    )
    out_ref[...] = mixed.astype(bf16)


VMEM = pl.BlockSpec(memory_space=pltpu.VMEM)
SMEM = pl.BlockSpec(memory_space=pltpu.SMEM)
ANY = pl.BlockSpec(memory_space=pl.ANY)


def columns_of(width, block):
    return pl.BlockSpec((width, H * DH), lambda i: (0, block))


def per_device(seq_size, head_size, tokens, w_proj, w_out, tile_user):
    rows, width = tokens.shape
    half = rows // 2
    tiles = rows // TILE
    blocks = seq_size * head_size
    seq, head = lax.axis_index("seq"), lax.axis_index("head")
    fold = H // head_size
    share = fold
    groups = seq_size // (fold * share)
    group, part, core = seq // (fold * share), (seq // share) % fold, seq % share
    me = part * head_size + head
    me_array = me.reshape(1).astype(jnp.int32)

    def partner(array, k):
        if k == 0:
            return array
        pairs = []
        for s in range(seq_size):
            for h in range(head_size):
                g, p, c = s // (fold * share), (s // share) % fold, s % share
                other = (p * head_size + h) ^ k
                t = (g * fold + other // head_size) * share + c
                pairs.append((s * head_size + h, t * head_size + other % head_size))
        return lax.ppermute(array, ("seq", "head"), pairs)

    def seq_flip(array, bit):
        return lax.ppermute(array, "seq", [(s, s ^ bit) for s in range(seq_size)])

    keys_sent = pl.pallas_call(
        project_keys,
        out_shape=[jax.ShapeDtypeStruct((rows, LANES), bf16)] * H,
        grid=(1,),
        in_specs=[SMEM, VMEM, columns_of(width, 1), columns_of(width, 3)],
        out_specs=[VMEM] * H,
        scratch_shapes=[pltpu.VMEM((H, rows, LANES), bf16)],
        name="project_keys",
    )(me_array, tokens, w_proj, w_proj)
    queries_sent = pl.pallas_call(
        project_queries,
        out_shape=[jax.ShapeDtypeStruct((half, LANES), bf16)] * H
        + [jax.ShapeDtypeStruct((rows, H * DH), bf16)],
        grid=(1,),
        in_specs=[SMEM, VMEM, columns_of(width, 2), columns_of(width, 0)],
        out_specs=[VMEM] * (H + 1),
        scratch_shapes=[pltpu.VMEM((H, half, LANES), bf16)],
        name="project_queries",
    )(me_array, tokens, w_proj, w_proj)
    gating = queries_sent[-1]

    index = jnp.arange(blocks, dtype=jnp.int32)
    block_head, block_seq = index % head_size, index // head_size
    block_core = block_seq % share
    block_me = (block_seq // share % fold) * head_size + block_head
    block_group = block_seq // (share * fold)
    from_me = jnp.bitwise_xor(block_me, me)
    asked = jnp.arange(H, dtype=jnp.int32) ^ me
    query_block = (
        (group * fold + asked // head_size) * share + core
    ) * head_size + asked % head_size
    start = jnp.sum((tile_user[None, :] < tile_user[:, None]).astype(jnp.int32), axis=1)
    length = jnp.sum((tile_user[None, :] == tile_user[:, None]).astype(f32), axis=1) * TILE

    def reach(first, last, query):
        return jnp.stack([jnp.asarray(v, jnp.int32) for v in (first, last, query)])

    arrived = [partner(keys_sent[k], k) for k in range(H)]
    last = arrived[-1]
    to_send, _ = lax.optimization_barrier((tuple(queries_sent[:H]), last))
    queries = jnp.stack([partner(to_send[k], k) for k in range(H)])
    if groups == 2 and share == 2:
        lots = [jnp.stack(arrived[:TEAM]), jnp.stack(arrived[TEAM:])]
        far = [seq_flip(lot, fold * share) for lot in lots]
        near = lots + [seq_flip(lot, 1) for lot in lots]
        far = far + [seq_flip(lot, 1) for lot in far]
        slot = jnp.bitwise_xor(block_core, core) * H + from_me
        tables = (start, 1.0 / length, query_block, slot)
        bound = group * (blocks // groups)
        totals = attend_call(tables, reach(bound, blocks, 0), queries, near, closes=False)
        size = totals.shape[0] // 2
        attention = [None] * H
        for begin in (TEAM, 0):
            team = attend_call(
                tables,
                reach(0, bound, begin),
                queries[begin : begin + TEAM],
                far,
                before=totals[size * (begin // TEAM) : size * (begin // TEAM + 1)],
            )
            for k in range(TEAM):
                attention[begin + k] = team[k]
    else:
        everything = lax.all_gather(jnp.stack(arrived), "seq", axis=0, tiled=True)
        tables = (start, 1.0 / length, query_block, block_seq * H + from_me)
        attention = attend_call(tables, reach(0, blocks, 0), queries, [everything])
    returned = jnp.stack([partner(attention[k], k) for k in range(H)])
    return pl.pallas_call(
        finish,
        out_shape=jax.ShapeDtypeStruct((rows, width), bf16),
        in_specs=[SMEM, VMEM, VMEM, VMEM, VMEM],
        out_specs=VMEM,
        name="finish",
    )(me_array, tokens, returned, gating, w_out)


def solution(mesh):
    placed = (P(("seq", "head"), None), P(), P(), P())
    return jax.shard_map(
        functools.partial(per_device, mesh.shape["seq"], mesh.shape["head"]),
        mesh=mesh,
        in_specs=placed,
        out_specs=P(("seq", "head"), None),
        check_vma=False,
    )
```

```python
import functools

import jax
import jax.numpy as jnp
from jax import lax
from jax.experimental import pallas as pl
from jax.experimental.pallas import tpu as pltpu
from jax.sharding import PartitionSpec as P

H = 8
DH = 64
TILE = 128
LANES = 2 * DH
TEAM = H // 2

epsilon = 1e-05

f32 = jnp.float32
bf16 = jnp.bfloat16


def layer_norm(values):
    center = values - jnp.mean(values, axis=-1, keepdims=True)
    spread = jnp.mean(center * center, axis=-1, keepdims=True)
    return center * lax.rsqrt(spread + epsilon)


def silu(values):
    half = values * 0.5
    return half + half * jnp.tanh(half)


def swap_halves(values):
    return pltpu.roll(values, DH, 1)


def low_lanes(rows):
    return lax.broadcasted_iota(jnp.int32, (rows, LANES), 1) < DH


def project(me_ref, tokens_ref, values_ref, queries_ref, keys_ref, *refs):
    outs, held = refs[:-1], refs[-1]
    rows = tokens_ref.shape[0]
    half = rows // 2
    normed = layer_norm(tokens_ref[...].astype(f32)).astype(bf16)
    low, half_low = low_lanes(rows), low_lanes(half)
    scale = 0.5 * DH ** (-0.5)
    keys = silu(jnp.dot(normed, keys_ref[...], preferred_element_type=f32))
    values = silu(jnp.dot(normed, values_ref[...], preferred_element_type=f32))
    queries = silu(jnp.dot(normed, queries_ref[...], preferred_element_type=f32)) * scale
    for pair in range(H // 2):
        at = slice(pair * LANES, (pair + 1) * LANES)
        key, value, upper, lower = keys[:, at], values[:, at], queries[:half, at], queries[half:, at]
        held[2 * pair, :rows] = jnp.where(low, key, swap_halves(value)).astype(bf16)
        held[2 * pair + 1, :rows] = jnp.where(low, swap_halves(key), value).astype(bf16)
        held[2 * pair, rows:] = jnp.where(half_low, upper, swap_halves(lower)).astype(bf16)
        held[2 * pair + 1, rows:] = jnp.where(half_low, swap_halves(upper), lower).astype(bf16)
    for k, out in enumerate(outs):
        out[...] = held[jnp.bitwise_xor(me_ref[0], k)]


def project_gating(tokens_ref, gating_weights, out_ref):
    normed = layer_norm(tokens_ref[...].astype(f32)).astype(bf16)
    gating = silu(jnp.dot(normed, gating_weights[...], preferred_element_type=f32))
    out_ref[...] = gating.astype(bf16)


def attend(
    opens, closes, reach_ref, start_ref, inverse_ref, block_ref, slot_ref, queries_ref, *refs
):
    step = pl.program_id(0)
    held, total, queries, sems = refs[-4:]
    out_ref = refs[-5]
    parts = refs[: -5 if opens else -6]
    rows = held.shape[1]
    half = rows // 2
    tiles = rows // TILE

    @pl.when(step == 0)
    def _():
        copies, at = [], 0
        for i, part in enumerate(parts):
            copies.append(
                pltpu.make_async_copy(part, held.at[pl.ds(at, part.shape[0])], sems.at[i])
            )
            at += part.shape[0]
        for copy in copies:
            copy.start()
        for copy in copies:
            copy.wait()

    low = low_lanes(half)
    blocks = [block_ref[reach_ref[2] + step * TEAM + i] for i in range(TEAM)]
    for i in range(TEAM):
        packed = queries_ref[i].astype(f32)
        queries[i * rows : i * rows + half] = jnp.where(low, packed, 0.0).astype(bf16)
        queries[i * rows + half : (i + 1) * rows] = jnp.where(
            low, swap_halves(packed), 0.0
        ).astype(bf16)
    starts = [start_ref[block * tiles + j] for block in blocks for j in range(tiles)]
    least, low_start, high_start = blocks[0], starts[0], starts[0]
    for block in blocks[1:]:
        least = jnp.minimum(least, block)
    for start in starts[1:]:
        low_start = jnp.minimum(low_start, start)
        high_start = jnp.maximum(high_start, start)
    total[...] = jnp.zeros_like(total) if opens else refs[-6][...]

    def add(key_block, count, masked):
        key_rows = [held[slot_ref[key_block + i]] for i in range(count)]
        key_rows = jnp.concatenate(key_rows, axis=0)
        if masked:
            column = lax.broadcasted_iota(jnp.int32, (TILE, count * rows), 1)
            ahead = column - lax.broadcasted_iota(jnp.int32, (TILE, count * rows), 0)
        def add_to(i):
            at = slice(i * rows, (i + 1) * rows)
            score = lax.dot_general(
                queries[at], key_rows, (((1,), (1,)), ((), ())), preferred_element_type=f32
            )
            weights = score + score * jnp.tanh(score)
            if masked:
                pieces = []
                for j in range(tiles):
                    from_start = starts[i * tiles + j] * TILE - key_block * rows
                    to_row = (blocks[i] - key_block) * rows + j * TILE
                    allowed = (column >= from_start) & (ahead <= to_row)
                    pieces.append(jnp.where(allowed, weights[j * TILE : (j + 1) * TILE], 0.0))
                weights = jnp.concatenate(pieces, axis=0)
            total[at] += jnp.dot(weights.astype(bf16), key_rows, preferred_element_type=f32)

        for i in range(TEAM):
            if masked:
                needed = starts[i * tiles] < (key_block + count) * tiles
                pl.when(needed)(functools.partial(add_to, i))
            else:
                add_to(i)

    def loop(begin, end, masked):
        def body(index, carry):
            add(index * TEAM, TEAM, masked)
            return carry

        lax.fori_loop(begin // TEAM, end // TEAM, body, 0)

    reach_low, reach_high = reach_ref[0], jnp.minimum(reach_ref[1], least)
    first = jnp.maximum(low_start // (tiles * TEAM) * TEAM, reach_low)
    whole = (high_start + tiles * TEAM - 1) // (tiles * TEAM) * TEAM
    whole = jnp.maximum(first, jnp.minimum(whole, reach_high))
    loop(first, jnp.minimum(whole, reach_high), True)
    loop(whole, reach_high, False)

    @pl.when(least < reach_ref[1])
    def _():
        add(least, TEAM, True)

    if not closes:
        out_ref[...] = total[...]
        return
    for i in range(TEAM):
        at = i * rows
        upper = total[at : at + half] * inverse_ref[blocks[i] * tiles]
        lower = total[at + half : at + rows] * inverse_ref[blocks[i] * tiles + tiles - 1]
        out_ref[i] = jnp.where(low, swap_halves(upper), lower).astype(bf16)


def attend_call(tables, reach, queries, parts, before=None, closes=True):
    half, rows = queries.shape[1], 2 * queries.shape[1]
    steps = queries.shape[0] // TEAM
    held_blocks = sum(array.shape[0] for array in parts)
    totals = pl.BlockSpec((TEAM * rows, LANES), lambda i, *_: (i, 0))
    packed = pl.BlockSpec((TEAM, half, LANES), lambda i, *_: (i, 0, 0))
    extra = [] if before is None else [before]
    return pl.pallas_call(
        functools.partial(attend, before is None, closes),
        grid_spec=pltpu.PrefetchScalarGridSpec(
            num_scalar_prefetch=5,
            grid=(steps,),
            in_specs=[packed] + [ANY] * len(parts) + [totals] * len(extra),
            out_specs=packed if closes else totals,
            scratch_shapes=[
                pltpu.VMEM((held_blocks, rows, LANES), bf16),
                pltpu.VMEM((TEAM * rows, LANES), f32),
                pltpu.VMEM((TEAM * rows, LANES), bf16),
                pltpu.SemaphoreType.DMA((len(parts),)),
            ],
        ),
        out_shape=jax.ShapeDtypeStruct(queries.shape, bf16)
        if closes
        else jax.ShapeDtypeStruct((steps * TEAM * rows, LANES), f32),
        compiler_params=pltpu.CompilerParams(vmem_limit_bytes=40 << 20),
        cost_estimate=pl.CostEstimate(
            flops=steps * 2_000_000_000, bytes_accessed=4_000_000, transcendentals=4_000_000
        ),
        name="attend",
    )(reach, *tables, queries, *parts, *extra)


def finish(me_ref, tokens_ref, attention_ref, gating_ref, weights_ref, out_ref):
    rows = tokens_ref.shape[0]
    half = rows // 2
    low = low_lanes(half)
    uppers, lowers = [], []
    for pair in range(H // 2):
        one = attention_ref[jnp.bitwise_xor(me_ref[0], 2 * pair)].astype(f32)
        two = attention_ref[jnp.bitwise_xor(me_ref[0], 2 * pair + 1)].astype(f32)
        uppers.append(jnp.where(low, one, swap_halves(two)))
        lowers.append(jnp.where(low, swap_halves(one), two))
    attention = jnp.concatenate(
        [jnp.concatenate(uppers, axis=1), jnp.concatenate(lowers, axis=1)], axis=0
    )
    gated = (layer_norm(attention) * gating_ref[...].astype(f32)).astype(bf16)
    mixed = tokens_ref[...].astype(f32) + jnp.dot(
        gated, weights_ref[...], preferred_element_type=f32
    )
    out_ref[...] = mixed.astype(bf16)


VMEM = pl.BlockSpec(memory_space=pltpu.VMEM)
SMEM = pl.BlockSpec(memory_space=pltpu.SMEM)
ANY = pl.BlockSpec(memory_space=pl.ANY)


def columns_of(width, block):
    return pl.BlockSpec((width, H * DH), lambda i: (0, block))


def per_device(seq_size, head_size, tokens, w_proj, w_out, tile_user):
    rows, width = tokens.shape
    half = rows // 2
    tiles = rows // TILE
    blocks = seq_size * head_size
    seq, head = lax.axis_index("seq"), lax.axis_index("head")
    fold = H // head_size
    share = fold
    groups = seq_size // (fold * share)
    group, part, core = seq // (fold * share), (seq // share) % fold, seq % share
    me = part * head_size + head
    me_array = me.reshape(1).astype(jnp.int32)

    def partner(array, k):
        if k == 0:
            return array
        pairs = []
        for s in range(seq_size):
            for h in range(head_size):
                g, p, c = s // (fold * share), (s // share) % fold, s % share
                other = (p * head_size + h) ^ k
                t = (g * fold + other // head_size) * share + c
                pairs.append((s * head_size + h, t * head_size + other % head_size))
        return lax.ppermute(array, ("seq", "head"), pairs)

    def seq_flip(array, bit):
        return lax.ppermute(array, "seq", [(s, s ^ bit) for s in range(seq_size)])

    sent = pl.pallas_call(
        project,
        out_shape=[jax.ShapeDtypeStruct((rows + half, LANES), bf16)] * H,
        grid=(1,),
        in_specs=[SMEM, VMEM] + [columns_of(width, i) for i in (1, 2, 3)],
        out_specs=[VMEM] * H,
        scratch_shapes=[pltpu.VMEM((H, rows + half, LANES), bf16)],
        name="project",
    )(me_array, tokens, w_proj, w_proj, w_proj)
    gating = pl.pallas_call(
        project_gating,
        out_shape=jax.ShapeDtypeStruct((rows, H * DH), bf16),
        grid=(1,),
        in_specs=[VMEM, columns_of(width, 0)],
        out_specs=VMEM,
        name="project_gating",
    )(tokens, w_proj)

    index = jnp.arange(blocks, dtype=jnp.int32)
    block_head, block_seq = index % head_size, index // head_size
    block_core = block_seq % share
    block_me = (block_seq // share % fold) * head_size + block_head
    block_group = block_seq // (share * fold)
    from_me = jnp.bitwise_xor(block_me, me)
    asked = jnp.arange(H, dtype=jnp.int32) ^ me
    query_block = (
        (group * fold + asked // head_size) * share + core
    ) * head_size + asked % head_size
    start = jnp.sum((tile_user[None, :] < tile_user[:, None]).astype(jnp.int32), axis=1)
    length = jnp.sum((tile_user[None, :] == tile_user[:, None]).astype(f32), axis=1) * TILE

    def reach(first, last, query):
        return jnp.stack([jnp.asarray(v, jnp.int32) for v in (first, last, query)])

    arrived = [partner(sent[k], k) for k in range(H)]
    queries = jnp.stack([array[rows:] for array in arrived])
    arrived = [array[:rows] for array in arrived]
    if groups == 2 and share == 2:
        lots = [jnp.stack(arrived[:TEAM]), jnp.stack(arrived[TEAM:])]
        far = [seq_flip(lot, fold * share) for lot in lots]
        near = lots + [seq_flip(lot, 1) for lot in lots]
        far = far + [seq_flip(lot, 1) for lot in far]
        slot = jnp.bitwise_xor(block_core, core) * H + from_me
        tables = (start, 1.0 / length, query_block, slot)
        bound = group * (blocks // groups)
        totals = attend_call(tables, reach(bound, blocks, 0), queries, near, closes=False)
        size = totals.shape[0] // 2
        attention = [None] * H
        for begin in (TEAM, 0):
            team = attend_call(
                tables,
                reach(0, bound, begin),
                queries[begin : begin + TEAM],
                far,
                before=totals[size * (begin // TEAM) : size * (begin // TEAM + 1)],
            )
            for k in range(TEAM):
                attention[begin + k] = team[k]
    else:
        everything = lax.all_gather(jnp.stack(arrived), "seq", axis=0, tiled=True)
        tables = (start, 1.0 / length, query_block, block_seq * H + from_me)
        attention = attend_call(tables, reach(0, blocks, 0), queries, [everything])
    returned = jnp.stack([partner(attention[k], k) for k in range(H)])
    return pl.pallas_call(
        finish,
        out_shape=jax.ShapeDtypeStruct((rows, width), bf16),
        in_specs=[SMEM, VMEM, VMEM, VMEM, VMEM],
        out_specs=VMEM,
        name="finish",
    )(me_array, tokens, returned, gating, w_out)


def solution(mesh):
    placed = (P(("seq", "head"), None), P(), P(), P())
    return jax.shard_map(
        functools.partial(per_device, mesh.shape["seq"], mesh.shape["head"]),
        mesh=mesh,
        in_specs=placed,
        out_specs=P(("seq", "head"), None),
        check_vma=False,
    )
```

```python
import functools

import jax
import jax.numpy as jnp
from jax import lax
from jax.experimental import pallas as pl
from jax.experimental.pallas import tpu as pltpu
from jax.sharding import PartitionSpec as P

H = 8
DH = 64
TILE = 128
LANES = 2 * DH
TEAM = H // 2

epsilon = 1e-05

f32 = jnp.float32
bf16 = jnp.bfloat16


def layer_norm(values):
    center = values - jnp.mean(values, axis=-1, keepdims=True)
    spread = jnp.mean(center * center, axis=-1, keepdims=True)
    return center * lax.rsqrt(spread + epsilon)


def silu(values):
    half = values * 0.5
    return half + half * jnp.tanh(half)


def swap_halves(values):
    return pltpu.roll(values, DH, 1)


def low_lanes(rows):
    return lax.broadcasted_iota(jnp.int32, (rows, LANES), 1) < DH


def project(me_ref, tokens_ref, values_ref, queries_ref, keys_ref, *refs):
    outs, held = refs[:-1], refs[-1]
    rows = tokens_ref.shape[0]
    half = rows // 2
    normed = layer_norm(tokens_ref[...].astype(f32)).astype(bf16)
    low, half_low = low_lanes(rows), low_lanes(half)
    scale = 0.5 * DH ** (-0.5)
    keys = silu(jnp.dot(normed, keys_ref[...], preferred_element_type=f32))
    values = silu(jnp.dot(normed, values_ref[...], preferred_element_type=f32))
    queries = silu(jnp.dot(normed, queries_ref[...], preferred_element_type=f32)) * scale
    for pair in range(H // 2):
        at = slice(pair * LANES, (pair + 1) * LANES)
        key, value, upper, lower = keys[:, at], values[:, at], queries[:half, at], queries[half:, at]
        held[2 * pair, :rows] = jnp.where(low, key, swap_halves(value)).astype(bf16)
        held[2 * pair + 1, :rows] = jnp.where(low, swap_halves(key), value).astype(bf16)
        held[2 * pair, rows:] = jnp.where(half_low, upper, swap_halves(lower)).astype(bf16)
        held[2 * pair + 1, rows:] = jnp.where(half_low, swap_halves(upper), lower).astype(bf16)
    for k, out in enumerate(outs):
        out[...] = held[jnp.bitwise_xor(me_ref[0], k)]


def project_gating(tokens_ref, gating_weights, out_ref):
    normed = layer_norm(tokens_ref[...].astype(f32)).astype(bf16)
    gating = silu(jnp.dot(normed, gating_weights[...], preferred_element_type=f32))
    out_ref[...] = gating.astype(bf16)


def attend(
    opens, closes, start_ref, inverse_ref, block_ref, team_ref, slot_ref, queries_ref, *refs
):
    step = pl.program_id(0)
    held, total, queries, sem = refs[-4:]
    out_ref, keys_ref = refs[-5], refs[0]
    rows = held.shape[1]
    half = rows // 2
    tiles = rows // TILE

    @pl.when(step == 0)
    def _():
        copy = pltpu.make_async_copy(keys_ref, held, sem)
        copy.start()
        copy.wait()

    low = low_lanes(half)
    blocks = [block_ref[step * TEAM + i] for i in range(TEAM)]
    for i in range(TEAM):
        packed = queries_ref[i].astype(f32)
        queries[i * rows : i * rows + half] = jnp.where(low, packed, 0.0).astype(bf16)
        queries[i * rows + half : (i + 1) * rows] = jnp.where(
            low, swap_halves(packed), 0.0
        ).astype(bf16)
    starts = [start_ref[block * tiles + j] for block in blocks for j in range(tiles)]
    least, low_start, high_start = blocks[0], starts[0], starts[0]
    for block in blocks[1:]:
        least = jnp.minimum(least, block)
    for start in starts[1:]:
        low_start = jnp.minimum(low_start, start)
        high_start = jnp.maximum(high_start, start)
    total[...] = jnp.zeros_like(total) if opens else refs[1][...]

    def add(team, key_block, masked, chosen):
        key_rows = jnp.concatenate([held[slot_ref[team * TEAM + i]] for i in range(TEAM)], axis=0)
        if masked:
            column = lax.broadcasted_iota(jnp.int32, (TILE, TEAM * rows), 1)
            ahead = column - lax.broadcasted_iota(jnp.int32, (TILE, TEAM * rows), 0)

        def add_to(i):
            at = slice(i * rows, (i + 1) * rows)
            score = lax.dot_general(
                queries[at], key_rows, (((1,), (1,)), ((), ())), preferred_element_type=f32
            )
            weights = score + score * jnp.tanh(score)
            if masked:
                pieces = []
                for j in range(tiles):
                    from_start = starts[i * tiles + j] * TILE - key_block * rows
                    to_row = (blocks[i] - key_block) * rows + j * TILE
                    allowed = (column >= from_start) & (ahead <= to_row)
                    pieces.append(jnp.where(allowed, weights[j * TILE : (j + 1) * TILE], 0.0))
                weights = jnp.concatenate(pieces, axis=0)
            total[at] += jnp.dot(weights.astype(bf16), key_rows, preferred_element_type=f32)

        for i in range(TEAM):
            if chosen:
                needed = starts[i * tiles] < (key_block + TEAM) * tiles
                pl.when(needed)(functools.partial(add_to, i))
            else:
                add_to(i)

    def one_team(team, carry):
        key_block = team_ref[team]
        before = (key_block < least) & ((key_block + TEAM) * tiles > low_start)
        whole = key_block * tiles >= high_start
        pl.when(before & whole)(lambda: add(team, key_block, False, False))
        pl.when(before & ~whole)(lambda: add(team, key_block, True, True))
        pl.when(key_block == least)(lambda: add(team, key_block, True, False))
        return carry

    lax.fori_loop(0, held.shape[0] // TEAM, one_team, 0)
    if not closes:
        out_ref[...] = total[...]
        return
    for i in range(TEAM):
        at = i * rows
        upper = total[at : at + half] * inverse_ref[blocks[i] * tiles]
        lower = total[at + half : at + rows] * inverse_ref[blocks[i] * tiles + tiles - 1]
        out_ref[i] = jnp.where(low, swap_halves(upper), lower).astype(out_ref.dtype)


def attend_call(tables, queries, keys, before=None, gives=None):
    half, rows = queries.shape[1], 2 * queries.shape[1]
    steps = queries.shape[0] // TEAM
    totals = pl.BlockSpec((TEAM * rows, LANES), lambda i, *_: (i, 0))
    packed = pl.BlockSpec((TEAM, half, LANES), lambda i, *_: (i, 0, 0))
    extra = [] if before is None else [before]
    return pl.pallas_call(
        functools.partial(attend, before is None, gives is not None),
        grid_spec=pltpu.PrefetchScalarGridSpec(
            num_scalar_prefetch=5,
            grid=(steps,),
            in_specs=[packed, ANY] + [totals] * len(extra),
            out_specs=totals if gives is None else packed,
            scratch_shapes=[
                pltpu.VMEM(keys.shape, bf16),
                pltpu.VMEM((TEAM * rows, LANES), f32),
                pltpu.VMEM((TEAM * rows, LANES), bf16),
                pltpu.SemaphoreType.DMA,
            ],
        ),
        out_shape=jax.ShapeDtypeStruct((steps * TEAM * rows, LANES), f32)
        if gives is None
        else jax.ShapeDtypeStruct(queries.shape, gives),
        compiler_params=pltpu.CompilerParams(vmem_limit_bytes=40 << 20),
        cost_estimate=pl.CostEstimate(
            flops=steps * 2_000_000_000, bytes_accessed=4_000_000, transcendentals=4_000_000
        ),
        name="attend",
    )(*tables, queries, keys, *extra)


def finish(me_ref, tokens_ref, attention_ref, gating_ref, weights_ref, out_ref):
    rows = tokens_ref.shape[0]
    half = rows // 2
    low = low_lanes(half)
    uppers, lowers = [], []
    for pair in range(H // 2):
        one = attention_ref[jnp.bitwise_xor(me_ref[0], 2 * pair)].astype(f32)
        two = attention_ref[jnp.bitwise_xor(me_ref[0], 2 * pair + 1)].astype(f32)
        uppers.append(jnp.where(low, one, swap_halves(two)))
        lowers.append(jnp.where(low, swap_halves(one), two))
    attention = jnp.concatenate(
        [jnp.concatenate(uppers, axis=1), jnp.concatenate(lowers, axis=1)], axis=0
    )
    gated = (layer_norm(attention) * gating_ref[...].astype(f32)).astype(bf16)
    mixed = tokens_ref[...].astype(f32) + jnp.dot(
        gated, weights_ref[...], preferred_element_type=f32
    )
    out_ref[...] = mixed.astype(bf16)


VMEM = pl.BlockSpec(memory_space=pltpu.VMEM)
SMEM = pl.BlockSpec(memory_space=pltpu.SMEM)
ANY = pl.BlockSpec(memory_space=pl.ANY)


def columns_of(width, block):
    return pl.BlockSpec((width, H * DH), lambda i: (0, block))


def per_device(seq_size, head_size, tokens, w_proj, w_out, tile_user):
    rows, width = tokens.shape
    half = rows // 2
    tiles = rows // TILE
    blocks = seq_size * head_size
    seq, head = lax.axis_index("seq"), lax.axis_index("head")
    fold = H // head_size
    share = fold
    groups = seq_size // (fold * share)
    group, part, core = seq // (fold * share), (seq // share) % fold, seq % share
    me = part * head_size + head
    me_array = me.reshape(1).astype(jnp.int32)

    def partner(array, k):
        if k == 0:
            return array
        pairs = []
        for s in range(seq_size):
            for h in range(head_size):
                g, p, c = s // (fold * share), (s // share) % fold, s % share
                other = (p * head_size + h) ^ k
                t = (g * fold + other // head_size) * share + c
                pairs.append((s * head_size + h, t * head_size + other % head_size))
        return lax.ppermute(array, ("seq", "head"), pairs)

    def seq_flip(array, bit):
        return lax.ppermute(array, "seq", [(s, s ^ bit) for s in range(seq_size)])

    sent = pl.pallas_call(
        project,
        out_shape=[jax.ShapeDtypeStruct((rows + half, LANES), bf16)] * H,
        grid=(1,),
        in_specs=[SMEM, VMEM] + [columns_of(width, i) for i in (1, 2, 3)],
        out_specs=[VMEM] * H,
        scratch_shapes=[pltpu.VMEM((H, rows + half, LANES), bf16)],
        name="project",
    )(me_array, tokens, w_proj, w_proj, w_proj)
    gating = pl.pallas_call(
        project_gating,
        out_shape=jax.ShapeDtypeStruct((rows, H * DH), bf16),
        grid=(1,),
        in_specs=[VMEM, columns_of(width, 0)],
        out_specs=VMEM,
        name="project_gating",
    )(tokens, w_proj)

    start = jnp.sum((tile_user[None, :] < tile_user[:, None]).astype(jnp.int32), axis=1)
    length = jnp.sum((tile_user[None, :] == tile_user[:, None]).astype(f32), axis=1) * TILE
    asked = jnp.arange(H, dtype=jnp.int32) ^ me

    def blocks_of(places, in_group, in_core):
        in_seq = (in_group * fold + places // head_size) * share + in_core
        return in_seq * head_size + places % head_size

    arrived = [partner(sent[k], k) for k in range(H)]
    queries = jnp.stack([array[rows:] for array in arrived])
    keys = jnp.stack([array[:rows] for array in arrived])
    first_places = jnp.arange(0, H, TEAM, dtype=jnp.int32)
    mine = blocks_of(asked, group, core)
    if groups == 2 and share == 2:
        far_keys = seq_flip(keys, fold * share)
        other_queries = seq_flip(queries, 1)
        others = blocks_of(asked, group, 1 - core)

        def tables(query_blocks, in_group):
            return start, 1.0 / length, query_blocks, blocks_of(first_places, in_group, core), asked

        totals = attend_call(
            tables(jnp.concatenate([others, mine]), group),
            jnp.concatenate([other_queries, queries]),
            keys,
        )
        size = totals.shape[0] // 2
        far_keys, totals = lax.optimization_barrier((far_keys, totals))
        theirs = attend_call(
            tables(others, 1 - group), other_queries, far_keys, totals[:size], bf16
        )
        theirs = seq_flip(theirs, 1)
        ours = attend_call(tables(mine, 1 - group), queries, far_keys, totals[size:], f32)
        attention = (ours + theirs.astype(f32)).astype(bf16)
    else:
        everything = lax.all_gather(keys, "seq", axis=0, tiled=True)
        index = jnp.arange(blocks, dtype=jnp.int32)
        slot = index // head_size * H + jnp.bitwise_xor(index % head_size, me)
        tables = (start, 1.0 / length, mine, index[::TEAM], slot)
        attention = attend_call(tables, queries, everything, gives=bf16)
    returned = jnp.stack([partner(attention[k], k) for k in range(H)])
    return pl.pallas_call(
        finish,
        out_shape=jax.ShapeDtypeStruct((rows, width), bf16),
        in_specs=[SMEM, VMEM, VMEM, VMEM, VMEM],
        out_specs=VMEM,
        name="finish",
    )(me_array, tokens, returned, gating, w_out)


def solution(mesh):
    placed = (P(("seq", "head"), None), P(), P(), P())
    return jax.shard_map(
        functools.partial(per_device, mesh.shape["seq"], mesh.shape["head"]),
        mesh=mesh,
        in_specs=placed,
        out_specs=P(("seq", "head"), None),
        check_vma=False,
    )
```

```python
import functools

import jax
import jax.numpy as jnp
from jax import lax
from jax.experimental import pallas as pl
from jax.experimental.pallas import tpu as pltpu
from jax.sharding import PartitionSpec as P

H = 8
DH = 64
TILE = 128
LANES = 2 * DH
TEAM = H // 2

epsilon = 1e-05

f32 = jnp.float32
bf16 = jnp.bfloat16


def layer_norm(values):
    center = values - jnp.mean(values, axis=-1, keepdims=True)
    spread = jnp.mean(center * center, axis=-1, keepdims=True)
    return center * lax.rsqrt(spread + epsilon)


def silu(values):
    half = values * 0.5
    return half + half * jnp.tanh(half)


def swap_halves(values):
    return pltpu.roll(values, DH, 1)


def low_lanes(rows):
    return lax.broadcasted_iota(jnp.int32, (rows, LANES), 1) < DH


def project(me_ref, tokens_ref, values_ref, queries_ref, keys_ref, *refs):
    key_outs, query_outs = refs[:H], refs[H : H + 2]
    held_keys, held_queries = refs[H + 2 :]
    rows = tokens_ref.shape[0]
    half = rows // 2
    normed = layer_norm(tokens_ref[...].astype(f32)).astype(bf16)
    low, half_low = low_lanes(rows), low_lanes(half)
    scale = 0.5 * DH ** (-0.5)
    keys = silu(jnp.dot(normed, keys_ref[...], preferred_element_type=f32))
    values = silu(jnp.dot(normed, values_ref[...], preferred_element_type=f32))
    queries = silu(jnp.dot(normed, queries_ref[...], preferred_element_type=f32)) * scale
    for pair in range(H // 2):
        at = slice(pair * LANES, (pair + 1) * LANES)
        key, value, upper, lower = keys[:, at], values[:, at], queries[:half, at], queries[half:, at]
        held_keys[2 * pair] = jnp.where(low, key, swap_halves(value)).astype(bf16)
        held_keys[2 * pair + 1] = jnp.where(low, swap_halves(key), value).astype(bf16)
        held_queries[2 * pair] = jnp.where(half_low, upper, swap_halves(lower)).astype(bf16)
        held_queries[2 * pair + 1] = jnp.where(half_low, swap_halves(upper), lower).astype(bf16)
    for k in range(H):
        place = jnp.bitwise_xor(me_ref[0], k)
        key_outs[k][...] = held_keys[place]
        query_outs[k // TEAM][k % TEAM] = held_queries[place]


def project_gating(tokens_ref, gating_weights, out_ref):
    normed = layer_norm(tokens_ref[...].astype(f32)).astype(bf16)
    gating = silu(jnp.dot(normed, gating_weights[...], preferred_element_type=f32))
    out_ref[...] = gating.astype(bf16)


def attend(
    opens, closes, start_ref, inverse_ref, block_ref, team_ref, slot_ref, queries_ref, *refs
):
    step = pl.program_id(0)
    held, total, queries, sem = refs[-4:]
    out_ref, keys_ref = refs[-5], refs[0]
    rows = held.shape[1]
    half = rows // 2
    tiles = rows // TILE

    @pl.when(step == 0)
    def _():
        copy = pltpu.make_async_copy(keys_ref, held, sem)
        copy.start()
        copy.wait()

    low = low_lanes(half)
    blocks = [block_ref[step * TEAM + i] for i in range(TEAM)]
    for i in range(TEAM):
        packed = queries_ref[i].astype(f32)
        queries[i * rows : i * rows + half] = jnp.where(low, packed, 0.0).astype(bf16)
        queries[i * rows + half : (i + 1) * rows] = jnp.where(
            low, swap_halves(packed), 0.0
        ).astype(bf16)
    starts = [start_ref[block * tiles + j] for block in blocks for j in range(tiles)]
    least, low_start, high_start = blocks[0], starts[0], starts[0]
    for block in blocks[1:]:
        least = jnp.minimum(least, block)
    for start in starts[1:]:
        low_start = jnp.minimum(low_start, start)
        high_start = jnp.maximum(high_start, start)
    total[...] = jnp.zeros_like(total) if opens else refs[1][...]

    def add(team, key_block, masked, chosen):
        key_rows = jnp.concatenate([held[slot_ref[team * TEAM + i]] for i in range(TEAM)], axis=0)
        if masked:
            column = lax.broadcasted_iota(jnp.int32, (TILE, TEAM * rows), 1)
            ahead = column - lax.broadcasted_iota(jnp.int32, (TILE, TEAM * rows), 0)

        def add_to(i):
            at = slice(i * rows, (i + 1) * rows)
            score = lax.dot_general(
                queries[at], key_rows, (((1,), (1,)), ((), ())), preferred_element_type=f32
            )
            weights = score + score * jnp.tanh(score)
            if masked:
                pieces = []
                for j in range(tiles):
                    from_start = starts[i * tiles + j] * TILE - key_block * rows
                    to_row = (blocks[i] - key_block) * rows + j * TILE
                    allowed = (column >= from_start) & (ahead <= to_row)
                    pieces.append(jnp.where(allowed, weights[j * TILE : (j + 1) * TILE], 0.0))
                weights = jnp.concatenate(pieces, axis=0)
            total[at] += jnp.dot(weights.astype(bf16), key_rows, preferred_element_type=f32)

        for i in range(TEAM):
            if chosen:
                needed = starts[i * tiles] < (key_block + TEAM) * tiles
                pl.when(needed)(functools.partial(add_to, i))
            else:
                add_to(i)

    def one_team(team, carry):
        key_block = team_ref[team]
        before = (key_block < least) & ((key_block + TEAM) * tiles > low_start)
        whole = key_block * tiles >= high_start
        pl.when(before & whole)(lambda: add(team, key_block, False, False))
        pl.when(before & ~whole)(lambda: add(team, key_block, True, True))
        pl.when(key_block == least)(lambda: add(team, key_block, True, False))
        return carry

    lax.fori_loop(0, held.shape[0] // TEAM, one_team, 0)
    if not closes:
        out_ref[...] = total[...]
        return
    for i in range(TEAM):
        at = i * rows
        upper = total[at : at + half] * inverse_ref[blocks[i] * tiles]
        lower = total[at + half : at + rows] * inverse_ref[blocks[i] * tiles + tiles - 1]
        out_ref[i] = jnp.where(low, swap_halves(upper), lower).astype(out_ref.dtype)


def attend_call(tables, queries, keys, before=None, gives=None):
    half, rows = queries.shape[1], 2 * queries.shape[1]
    steps = queries.shape[0] // TEAM
    totals = pl.BlockSpec((TEAM * rows, LANES), lambda i, *_: (i, 0))
    packed = pl.BlockSpec((TEAM, half, LANES), lambda i, *_: (i, 0, 0))
    extra = [] if before is None else [before]
    return pl.pallas_call(
        functools.partial(attend, before is None, gives is not None),
        grid_spec=pltpu.PrefetchScalarGridSpec(
            num_scalar_prefetch=5,
            grid=(steps,),
            in_specs=[packed, ANY] + [totals] * len(extra),
            out_specs=totals if gives is None else packed,
            scratch_shapes=[
                pltpu.VMEM(keys.shape, bf16),
                pltpu.VMEM((TEAM * rows, LANES), f32),
                pltpu.VMEM((TEAM * rows, LANES), bf16),
                pltpu.SemaphoreType.DMA,
            ],
        ),
        out_shape=jax.ShapeDtypeStruct((steps * TEAM * rows, LANES), f32)
        if gives is None
        else jax.ShapeDtypeStruct(queries.shape, gives),
        compiler_params=pltpu.CompilerParams(vmem_limit_bytes=24 << 20),
        cost_estimate=pl.CostEstimate(
            flops=steps * 2_000_000_000, bytes_accessed=4_000_000, transcendentals=4_000_000
        ),
        name="attend",
    )(*tables, queries, keys, *extra)


def finish(me_ref, tokens_ref, attention_ref, gating_ref, weights_ref, out_ref):
    rows = tokens_ref.shape[0]
    half = rows // 2
    low = low_lanes(half)
    uppers, lowers = [], []
    for pair in range(H // 2):
        one = attention_ref[jnp.bitwise_xor(me_ref[0], 2 * pair)].astype(f32)
        two = attention_ref[jnp.bitwise_xor(me_ref[0], 2 * pair + 1)].astype(f32)
        uppers.append(jnp.where(low, one, swap_halves(two)))
        lowers.append(jnp.where(low, swap_halves(one), two))
    attention = jnp.concatenate(
        [jnp.concatenate(uppers, axis=1), jnp.concatenate(lowers, axis=1)], axis=0
    )
    gated = (layer_norm(attention) * gating_ref[...].astype(f32)).astype(bf16)
    mixed = tokens_ref[...].astype(f32) + jnp.dot(
        gated, weights_ref[...], preferred_element_type=f32
    )
    out_ref[...] = mixed.astype(bf16)


VMEM = pl.BlockSpec(memory_space=pltpu.VMEM)
SMEM = pl.BlockSpec(memory_space=pltpu.SMEM)
ANY = pl.BlockSpec(memory_space=pl.ANY)


def columns_of(width, block):
    return pl.BlockSpec((width, H * DH), lambda i: (0, block))


def per_device(seq_size, head_size, tokens, w_proj, w_out, tile_user):
    rows, width = tokens.shape
    half = rows // 2
    tiles = rows // TILE
    blocks = seq_size * head_size
    seq, head = lax.axis_index("seq"), lax.axis_index("head")
    fold = H // head_size
    share = fold
    groups = seq_size // (fold * share)
    group, part, core = seq // (fold * share), (seq // share) % fold, seq % share
    me = part * head_size + head
    me_array = me.reshape(1).astype(jnp.int32)

    def partner(array, k):
        if k == 0:
            return array
        pairs = []
        for s in range(seq_size):
            for h in range(head_size):
                g, p, c = s // (fold * share), (s // share) % fold, s % share
                other = (p * head_size + h) ^ k
                t = (g * fold + other // head_size) * share + c
                pairs.append((s * head_size + h, t * head_size + other % head_size))
        return lax.ppermute(array, ("seq", "head"), pairs)

    def seq_flip(array, bit):
        return lax.ppermute(array, "seq", [(s, s ^ bit) for s in range(seq_size)])

    *sent, queries_a, queries_b = pl.pallas_call(
        project,
        out_shape=[jax.ShapeDtypeStruct((rows, LANES), bf16)] * H
        + [jax.ShapeDtypeStruct((TEAM, half, LANES), bf16)] * 2,
        grid=(1,),
        in_specs=[SMEM, VMEM] + [columns_of(width, i) for i in (1, 2, 3)],
        out_specs=[VMEM] * (H + 2),
        scratch_shapes=[pltpu.VMEM((H, rows, LANES), bf16), pltpu.VMEM((H, half, LANES), bf16)],
        compiler_params=pltpu.CompilerParams(vmem_limit_bytes=12 << 20),
        name="project",
    )(me_array, tokens, w_proj, w_proj, w_proj)
    gating = pl.pallas_call(
        project_gating,
        out_shape=jax.ShapeDtypeStruct((rows, H * DH), bf16),
        grid=(1,),
        in_specs=[VMEM, columns_of(width, 0)],
        out_specs=VMEM,
        compiler_params=pltpu.CompilerParams(vmem_limit_bytes=12 << 20),
        name="project_gating",
    )(tokens, w_proj)

    start = jnp.sum((tile_user[None, :] < tile_user[:, None]).astype(jnp.int32), axis=1)
    length = jnp.sum((tile_user[None, :] == tile_user[:, None]).astype(f32), axis=1) * TILE
    asked = jnp.arange(H, dtype=jnp.int32) ^ me

    def blocks_of(places, in_group, in_core):
        in_seq = (in_group * fold + places // head_size) * share + in_core
        return in_seq * head_size + places % head_size

    def exchange(near, far):
        got = [(near[0], far[0])]
        for k in range(1, TEAM):
            both = partner(jnp.stack([near[k], far[k]]), k)
            got.append((both[0], both[1]))
        return jnp.stack([pair[0] for pair in got] + [pair[1] for pair in got])

    queries_b = partner(queries_b, TEAM)
    arrived = [partner(sent[k], k) for k in range(H)]
    queries_a, queries_b, _ = lax.optimization_barrier((queries_a, queries_b, arrived[-1]))
    queries = exchange(queries_a, queries_b)
    keys = jnp.stack(arrived)
    first_places = jnp.arange(0, H, TEAM, dtype=jnp.int32)
    mine = blocks_of(asked, group, core)
    if groups == 2 and share == 2:
        far_keys = seq_flip(keys, fold * share)
        other_queries = seq_flip(queries, 1)
        others = blocks_of(asked, group, 1 - core)

        def tables(query_blocks, in_group):
            return start, 1.0 / length, query_blocks, blocks_of(first_places, in_group, core), asked

        near_ours = attend_call(tables(mine, group), queries, keys)
        near_theirs = attend_call(tables(others, group), other_queries, keys)
        size = near_ours.shape[0] // 2
        far_keys, near_theirs, near_ours, gating = lax.optimization_barrier(
            (far_keys, near_theirs, near_ours, gating)
        )
        theirs = attend_call(
            tables(others, 1 - group), other_queries, far_keys, near_theirs, bf16
        )
        theirs = seq_flip(theirs, 1)
        team_b = attend_call(
            tables(mine[TEAM:], 1 - group), queries[TEAM:], far_keys, near_ours[size:], f32
        )
        attention_b = (team_b + theirs[TEAM:].astype(f32)).astype(bf16)
        attention_b, totals_a = lax.optimization_barrier((attention_b, near_ours[:size]))
        team_a = attend_call(
            tables(mine[:TEAM], 1 - group), queries[:TEAM], far_keys, totals_a, f32
        )
        attention_a = (team_a + theirs[:TEAM].astype(f32)).astype(bf16)
    else:
        everything = lax.all_gather(keys, "seq", axis=0, tiled=True)
        index = jnp.arange(blocks, dtype=jnp.int32)
        slot = index // head_size * H + jnp.bitwise_xor(index % head_size, me)
        tables = (start, 1.0 / length, mine, index[::TEAM], slot)
        attention = attend_call(tables, queries, everything, gives=bf16)
        attention_a, attention_b = attention[:TEAM], attention[TEAM:]
    returned = exchange(attention_a, partner(attention_b, TEAM))
    return pl.pallas_call(
        finish,
        out_shape=jax.ShapeDtypeStruct((rows, width), bf16),
        in_specs=[SMEM, VMEM, VMEM, VMEM, VMEM],
        out_specs=VMEM,
        compiler_params=pltpu.CompilerParams(vmem_limit_bytes=12 << 20),
        name="finish",
    )(me_array, tokens, returned, gating, w_out)


def solution(mesh):
    placed = (P(("seq", "head"), None), P(), P(), P())
    return jax.shard_map(
        functools.partial(per_device, mesh.shape["seq"], mesh.shape["head"]),
        mesh=mesh,
        in_specs=placed,
        out_specs=P(("seq", "head"), None),
        check_vma=False,
    )
```

```python
import functools

import jax
import jax.numpy as jnp
from jax import lax
from jax.experimental import pallas as pl
from jax.experimental.pallas import tpu as pltpu
from jax.sharding import PartitionSpec as P

H = 8
DH = 64
TILE = 128
LANES = 2 * DH
TEAM = H // 2

epsilon = 1e-05

f32 = jnp.float32
bf16 = jnp.bfloat16


def layer_norm(values):
    center = values - jnp.mean(values, axis=-1, keepdims=True)
    spread = jnp.mean(center * center, axis=-1, keepdims=True)
    return center * lax.rsqrt(spread + epsilon)


def silu(values):
    half = values * 0.5
    return half + half * jnp.tanh(half)


def swap_halves(values):
    return pltpu.roll(values, DH, 1)


def low_lanes(rows):
    return lax.broadcasted_iota(jnp.int32, (rows, LANES), 1) < DH


def project(me_ref, tokens_ref, weights_ref, *refs):
    outs, (tokens, weights, held, sems) = refs[:-4], refs[-4:]
    rows = tokens.shape[0]
    half = rows // 2
    copies = [pltpu.make_async_copy(tokens_ref, tokens, sems.at[0])]
    for i, block in enumerate((3, 1, 2)):
        at = pl.ds(block * H * DH, H * DH)
        copies.append(
            pltpu.make_async_copy(weights_ref.at[:, at], weights.at[i], sems.at[i + 1])
        )
    for copy in copies:
        copy.start()
    copies[0].wait()
    normed = layer_norm(tokens[...].astype(f32)).astype(bf16)
    low, half_low = low_lanes(rows), low_lanes(half)
    scale = 0.5 * DH ** (-0.5)
    copies[1].wait()
    keys = silu(jnp.dot(normed, weights[0], preferred_element_type=f32))
    copies[2].wait()
    values = silu(jnp.dot(normed, weights[1], preferred_element_type=f32))
    copies[3].wait()
    queries = silu(jnp.dot(normed, weights[2], preferred_element_type=f32)) * scale
    for pair in range(H // 2):
        at = slice(pair * LANES, (pair + 1) * LANES)
        key, value, upper, lower = keys[:, at], values[:, at], queries[:half, at], queries[half:, at]
        held[2 * pair, :rows] = jnp.where(low, key, swap_halves(value)).astype(bf16)
        held[2 * pair + 1, :rows] = jnp.where(low, swap_halves(key), value).astype(bf16)
        held[2 * pair, rows:] = jnp.where(half_low, upper, swap_halves(lower)).astype(bf16)
        held[2 * pair + 1, rows:] = jnp.where(half_low, swap_halves(upper), lower).astype(bf16)
    for k, out in enumerate(outs):
        out[...] = held[jnp.bitwise_xor(me_ref[0], k)]


def project_gating(tokens_ref, weights_ref, out_ref, tokens, weights, sems):
    copies = [
        pltpu.make_async_copy(tokens_ref, tokens, sems.at[0]),
        pltpu.make_async_copy(weights_ref.at[:, pl.ds(0, H * DH)], weights, sems.at[1]),
    ]
    for copy in copies:
        copy.start()
    for copy in copies:
        copy.wait()
    normed = layer_norm(tokens[...].astype(f32)).astype(bf16)
    gating = silu(jnp.dot(normed, weights[...], preferred_element_type=f32))
    out_ref[...] = gating.astype(bf16)


def attend(
    start_ref, inverse_ref, block_ref, team_ref, slot_ref, queries_ref, held, *refs
):
    step = pl.program_id(0)
    *before, out_ref, total, queries = refs
    rows = held.shape[1]
    half = rows // 2
    tiles = rows // TILE
    low = low_lanes(half)
    blocks = [block_ref[step * TEAM + i] for i in range(TEAM)]
    for i in range(TEAM):
        packed = queries_ref[i].astype(f32)
        queries[i * rows : i * rows + half] = jnp.where(low, packed, 0.0).astype(bf16)
        queries[i * rows + half : (i + 1) * rows] = jnp.where(
            low, swap_halves(packed), 0.0
        ).astype(bf16)
    starts = [start_ref[block * tiles + j] for block in blocks for j in range(tiles)]
    least, low_start, high_start, high_first = blocks[0], starts[0], starts[0], starts[0]
    for block in blocks[1:]:
        least = jnp.minimum(least, block)
    for start in starts[1:]:
        low_start = jnp.minimum(low_start, start)
        high_start = jnp.maximum(high_start, start)
    for start in starts[tiles::tiles]:
        high_first = jnp.maximum(high_first, start)
    total[...] = jnp.zeros_like(total)

    def add(team, key_block, masked, chosen):
        key_rows = jnp.concatenate([held[slot_ref[team * TEAM + i]] for i in range(TEAM)], axis=0)
        if masked:
            column = lax.broadcasted_iota(jnp.int32, (TILE, TEAM * rows), 1)
            ahead = column - lax.broadcasted_iota(jnp.int32, (TILE, TEAM * rows), 0)

        def add_to(i):
            at = slice(i * rows, (i + 1) * rows)
            score = lax.dot_general(
                queries[at], key_rows, (((1,), (1,)), ((), ())), preferred_element_type=f32
            )
            weights = score + score * jnp.tanh(score)
            if masked:
                pieces = []
                for j in range(tiles):
                    from_start = starts[i * tiles + j] * TILE - key_block * rows
                    to_row = (blocks[i] - key_block) * rows + j * TILE
                    allowed = (column >= from_start) & (ahead <= to_row)
                    pieces.append(jnp.where(allowed, weights[j * TILE : (j + 1) * TILE], 0.0))
                weights = jnp.concatenate(pieces, axis=0)
            total[at] += jnp.dot(weights.astype(bf16), key_rows, preferred_element_type=f32)

        for i in range(TEAM):
            if chosen:
                needed = starts[i * tiles] < (key_block + TEAM) * tiles
                pl.when(needed)(functools.partial(add_to, i))
            else:
                add_to(i)

    def one_team(team, carry):
        key_block = team_ref[team]
        earlier = (key_block < least) & ((key_block + TEAM) * tiles > low_start)
        whole = key_block * tiles >= high_start
        every = (key_block + TEAM) * tiles > high_first
        pl.when(earlier & whole)(lambda: add(team, key_block, False, False))
        pl.when(earlier & ~every)(lambda: add(team, key_block, True, True))
        pl.when((earlier & ~whole & every) | (key_block == least))(
            lambda: add(team, key_block, True, False)
        )
        return carry

    lax.fori_loop(0, held.shape[0] // TEAM, one_team, 0)
    for i in range(TEAM):
        at = i * rows
        upper = total[at : at + half] * inverse_ref[blocks[i] * tiles]
        lower = total[at + half : at + rows] * inverse_ref[blocks[i] * tiles + tiles - 1]
        packed = jnp.where(low, swap_halves(upper), lower)
        for more in before:
            packed = packed + more[i].astype(f32)
        out_ref[i] = packed.astype(out_ref.dtype)


def attend_call(tables, queries, keys, gives, *before):
    half, rows = queries.shape[1], 2 * queries.shape[1]
    steps = queries.shape[0] // TEAM
    packed = pl.BlockSpec((TEAM, half, LANES), lambda i, *_: (i, 0, 0))
    return pl.pallas_call(
        attend,
        grid_spec=pltpu.PrefetchScalarGridSpec(
            num_scalar_prefetch=5,
            grid=(steps,),
            in_specs=[
                packed,
                pl.BlockSpec(keys.shape, lambda i, *_: (0, 0, 0), pipeline_mode=pl.Buffered(1)),
            ]
            + [packed] * len(before),
            out_specs=packed,
            scratch_shapes=[
                pltpu.VMEM((TEAM * rows, LANES), f32),
                pltpu.VMEM((TEAM * rows, LANES), bf16),
            ],
        ),
        out_shape=jax.ShapeDtypeStruct(queries.shape, gives),
        compiler_params=pltpu.CompilerParams(vmem_limit_bytes=24 << 20),
        cost_estimate=pl.CostEstimate(
            flops=steps * 2_000_000_000, bytes_accessed=4_000_000, transcendentals=4_000_000
        ),
        name="attend",
    )(*tables, queries, keys, *before)


def finish(me_ref, tokens_ref, attention_ref, gating_ref, weights_ref, out_ref):
    rows = tokens_ref.shape[0]
    half = rows // 2
    low = low_lanes(half)
    uppers, lowers = [], []
    for pair in range(H // 2):
        one = attention_ref[jnp.bitwise_xor(me_ref[0], 2 * pair)].astype(f32)
        two = attention_ref[jnp.bitwise_xor(me_ref[0], 2 * pair + 1)].astype(f32)
        uppers.append(jnp.where(low, one, swap_halves(two)))
        lowers.append(jnp.where(low, swap_halves(one), two))
    attention = jnp.concatenate(
        [jnp.concatenate(uppers, axis=1), jnp.concatenate(lowers, axis=1)], axis=0
    )
    gated = (layer_norm(attention) * gating_ref[...].astype(f32)).astype(bf16)
    mixed = tokens_ref[...].astype(f32) + jnp.dot(
        gated, weights_ref[...], preferred_element_type=f32
    )
    out_ref[...] = mixed.astype(bf16)


VMEM = pl.BlockSpec(memory_space=pltpu.VMEM)
SMEM = pl.BlockSpec(memory_space=pltpu.SMEM)
HBM = pl.BlockSpec(memory_space=pltpu.HBM)


def per_device(seq_size, head_size, tokens, w_proj, w_out, tile_user):
    rows, width = tokens.shape
    half = rows // 2
    tiles = rows // TILE
    blocks = seq_size * head_size
    seq, head = lax.axis_index("seq"), lax.axis_index("head")
    fold = H // head_size
    share = fold
    groups = seq_size // (fold * share)
    group, part, core = seq // (fold * share), (seq // share) % fold, seq % share
    me = part * head_size + head
    me_array = me.reshape(1).astype(jnp.int32)

    def partner(array, k):
        if k == 0:
            return array
        pairs = []
        for s in range(seq_size):
            for h in range(head_size):
                g, p, c = s // (fold * share), (s // share) % fold, s % share
                other = (p * head_size + h) ^ k
                t = (g * fold + other // head_size) * share + c
                pairs.append((s * head_size + h, t * head_size + other % head_size))
        return lax.ppermute(array, ("seq", "head"), pairs)

    def seq_flip(array, bit):
        return lax.ppermute(array, "seq", [(s, s ^ bit) for s in range(seq_size)])

    sent = pl.pallas_call(
        project,
        out_shape=[jax.ShapeDtypeStruct((rows + half, LANES), bf16)] * H,
        in_specs=[SMEM, HBM, HBM],
        out_specs=[VMEM] * H,
        scratch_shapes=[
            pltpu.VMEM((rows, width), bf16),
            pltpu.VMEM((3, width, H * DH), bf16),
            pltpu.VMEM((H, rows + half, LANES), bf16),
            pltpu.SemaphoreType.DMA((4,)),
        ],
        compiler_params=pltpu.CompilerParams(vmem_limit_bytes=58 << 20),
        name="project",
    )(me_array, tokens, w_proj)
    def gating_of(tokens):
        return pl.pallas_call(
            project_gating,
            out_shape=jax.ShapeDtypeStruct((rows, H * DH), bf16),
            in_specs=[HBM, HBM],
            out_specs=VMEM,
            scratch_shapes=[
                pltpu.VMEM((rows, width), bf16),
                pltpu.VMEM((width, H * DH), bf16),
                pltpu.SemaphoreType.DMA((2,)),
            ],
            compiler_params=pltpu.CompilerParams(vmem_limit_bytes=12 << 20),
            name="project_gating",
        )(tokens, w_proj)

    start = jnp.sum((tile_user[None, :] < tile_user[:, None]).astype(jnp.int32), axis=1)
    length = jnp.sum((tile_user[None, :] == tile_user[:, None]).astype(f32), axis=1) * TILE
    asked = jnp.arange(H, dtype=jnp.int32) ^ me

    def blocks_of(places, in_group, in_core):
        in_seq = (in_group * fold + places // head_size) * share + in_core
        return in_seq * head_size + places % head_size

    def exchange(near, far):
        got = [(near[0], far[0])]
        for k in range(1, TEAM):
            both = partner(jnp.stack([near[k], far[k]]), k)
            got.append((both[0], both[1]))
        return jnp.stack([pair[0] for pair in got] + [pair[1] for pair in got])

    arrived = [partner(sent[k], k) for k in range(H)]
    queries = jnp.stack([array[rows:] for array in arrived])
    keys = jnp.stack([array[:rows] for array in arrived])
    first_places = jnp.arange(0, H, TEAM, dtype=jnp.int32)
    mine = blocks_of(asked, group, core)
    if groups == 2 and share == 2:
        far_keys = seq_flip(keys, fold * share)
        other_queries = seq_flip(queries, 1)
        others = blocks_of(asked, group, 1 - core)

        def tables(query_blocks, in_group):
            return start, 1.0 / length, query_blocks, blocks_of(first_places, in_group, core), asked

        near_ours = attend_call(tables(mine, group), queries, keys, f32)
        near_theirs = attend_call(tables(others, group), other_queries, keys, f32)
        gating = gating_of(lax.optimization_barrier((tokens, near_theirs))[0])
        far_keys, near_theirs, near_ours, gating = lax.optimization_barrier(
            (far_keys, near_theirs, near_ours, gating)
        )
        theirs = attend_call(
            tables(others, 1 - group), other_queries, far_keys, bf16, near_theirs
        )
        theirs = seq_flip(theirs, 1)
        team_b = attend_call(
            tables(mine[TEAM:], 1 - group), queries[TEAM:], far_keys, f32, near_ours[TEAM:]
        )
        attention_b = (team_b + theirs[TEAM:].astype(f32)).astype(bf16)
        attention_b, near_a = lax.optimization_barrier((attention_b, near_ours[:TEAM]))
        attention_a = attend_call(
            tables(mine[:TEAM], 1 - group), queries[:TEAM], far_keys, bf16, near_a, theirs[:TEAM]
        )
    else:
        everything = lax.all_gather(keys, "seq", axis=0, tiled=True)
        index = jnp.arange(blocks, dtype=jnp.int32)
        slot = index // head_size * H + jnp.bitwise_xor(index % head_size, me)
        tables = (start, 1.0 / length, mine, index[::TEAM], slot)
        attention = attend_call(tables, queries, everything, bf16)
        attention_a, attention_b = attention[:TEAM], attention[TEAM:]
        gating = gating_of(tokens)
    returned = exchange(attention_a, partner(attention_b, TEAM))
    return pl.pallas_call(
        finish,
        out_shape=jax.ShapeDtypeStruct((rows, width), bf16),
        in_specs=[SMEM, VMEM, VMEM, VMEM, VMEM],
        out_specs=VMEM,
        compiler_params=pltpu.CompilerParams(vmem_limit_bytes=12 << 20),
        name="finish",
    )(me_array, tokens, returned, gating, w_out)


def solution(mesh):
    placed = (P(("seq", "head"), None), P(), P(), P())
    return jax.shard_map(
        functools.partial(per_device, mesh.shape["seq"], mesh.shape["head"]),
        mesh=mesh,
        in_specs=placed,
        out_specs=P(("seq", "head"), None),
        check_vma=False,
    )
```

```python
import functools

import jax
import jax.numpy as jnp
from jax import lax
from jax.experimental import pallas as pl
from jax.experimental.pallas import tpu as pltpu
from jax.sharding import PartitionSpec as P

H = 8
DH = 64
TILE = 128
LANES = 2 * DH
TEAM = H // 2

epsilon = 1e-05

f32 = jnp.float32
bf16 = jnp.bfloat16


def layer_norm(values):
    center = values - jnp.mean(values, axis=-1, keepdims=True)
    spread = jnp.mean(center * center, axis=-1, keepdims=True)
    return center * lax.rsqrt(spread + epsilon)


def silu(values):
    half = values * 0.5
    return half + half * jnp.tanh(half)


def swap_halves(values):
    return pltpu.roll(values, DH, 1)


def low_lanes(rows):
    return lax.broadcasted_iota(jnp.int32, (rows, LANES), 1) < DH


def project(me_ref, tokens_ref, weights_ref, *refs):
    outs, (tokens, weights, held, sems) = refs[:-4], refs[-4:]
    rows = tokens.shape[0]
    half = rows // 2
    copies = [pltpu.make_async_copy(tokens_ref, tokens, sems.at[0])]
    for i, block in enumerate((3, 1, 2)):
        at = pl.ds(block * H * DH, H * DH)
        copies.append(
            pltpu.make_async_copy(weights_ref.at[:, at], weights.at[i], sems.at[i + 1])
        )
    for copy in copies:
        copy.start()
    copies[0].wait()
    normed = layer_norm(tokens[...].astype(f32)).astype(bf16)
    low, half_low = low_lanes(rows), low_lanes(half)
    scale = 0.5 * DH ** (-0.5)
    copies[1].wait()
    keys = silu(jnp.dot(normed, weights[0], preferred_element_type=f32))
    copies[2].wait()
    values = silu(jnp.dot(normed, weights[1], preferred_element_type=f32))
    copies[3].wait()
    queries = silu(jnp.dot(normed, weights[2], preferred_element_type=f32)) * scale
    for pair in range(H // 2):
        at = slice(pair * LANES, (pair + 1) * LANES)
        key, value, upper, lower = keys[:, at], values[:, at], queries[:half, at], queries[half:, at]
        held[2 * pair, :rows] = jnp.where(low, key, swap_halves(value)).astype(bf16)
        held[2 * pair + 1, :rows] = jnp.where(low, swap_halves(key), value).astype(bf16)
        held[2 * pair, rows:] = jnp.where(half_low, upper, swap_halves(lower)).astype(bf16)
        held[2 * pair + 1, rows:] = jnp.where(half_low, swap_halves(upper), lower).astype(bf16)
    for k, out in enumerate(outs):
        out[...] = held[jnp.bitwise_xor(me_ref[0], k)]


def project_gating(tokens_ref, weights_ref, out_ref, tokens, weights, sems):
    copies = [
        pltpu.make_async_copy(tokens_ref, tokens, sems.at[0]),
        pltpu.make_async_copy(weights_ref.at[:, pl.ds(0, H * DH)], weights, sems.at[1]),
    ]
    for copy in copies:
        copy.start()
    for copy in copies:
        copy.wait()
    normed = layer_norm(tokens[...].astype(f32)).astype(bf16)
    gating = silu(jnp.dot(normed, weights[...], preferred_element_type=f32))
    out_ref[...] = gating.astype(bf16)


def attend(
    start_ref, inverse_ref, block_ref, team_ref, slot_ref, queries_ref, held, *refs
):
    step = pl.program_id(0)
    *before, out_ref, total, queries = refs
    rows = held.shape[1]
    half = rows // 2
    tiles = rows // TILE
    low = low_lanes(half)
    blocks = [block_ref[step * TEAM + i] for i in range(TEAM)]
    for i in range(TEAM):
        packed = queries_ref[i].astype(f32)
        queries[i * rows : i * rows + half] = jnp.where(low, packed, 0.0).astype(bf16)
        queries[i * rows + half : (i + 1) * rows] = jnp.where(
            low, swap_halves(packed), 0.0
        ).astype(bf16)
    starts = [start_ref[block * tiles + j] for block in blocks for j in range(tiles)]
    least, low_start, high_start, high_first = blocks[0], starts[0], starts[0], starts[0]
    for block in blocks[1:]:
        least = jnp.minimum(least, block)
    for start in starts[1:]:
        low_start = jnp.minimum(low_start, start)
        high_start = jnp.maximum(high_start, start)
    for start in starts[tiles::tiles]:
        high_first = jnp.maximum(high_first, start)
    total[...] = jnp.zeros_like(total)

    def add(team, key_block, masked, chosen):
        key_rows = jnp.concatenate([held[slot_ref[team * TEAM + i]] for i in range(TEAM)], axis=0)
        if masked:
            column = lax.broadcasted_iota(jnp.int32, (TILE, TEAM * rows), 1)
            ahead = column - lax.broadcasted_iota(jnp.int32, (TILE, TEAM * rows), 0)

        def add_to(i):
            at = slice(i * rows, (i + 1) * rows)
            score = lax.dot_general(
                queries[at], key_rows, (((1,), (1,)), ((), ())), preferred_element_type=f32
            )
            weights = score + score * jnp.tanh(score)
            if masked:
                pieces = []
                for j in range(tiles):
                    from_start = starts[i * tiles + j] * TILE - key_block * rows
                    to_row = (blocks[i] - key_block) * rows + j * TILE
                    allowed = (column >= from_start) & (ahead <= to_row)
                    pieces.append(jnp.where(allowed, weights[j * TILE : (j + 1) * TILE], 0.0))
                weights = jnp.concatenate(pieces, axis=0)
            total[at] += jnp.dot(weights.astype(bf16), key_rows, preferred_element_type=f32)

        for i in range(TEAM):
            if chosen:
                needed = starts[i * tiles] < (key_block + TEAM) * tiles
                pl.when(needed)(functools.partial(add_to, i))
            else:
                add_to(i)

    def one_team(team, carry):
        key_block = team_ref[team]
        earlier = (key_block < least) & ((key_block + TEAM) * tiles > low_start)
        whole = key_block * tiles >= high_start
        every = (key_block + TEAM) * tiles > high_first
        pl.when(earlier & whole)(lambda: add(team, key_block, False, False))
        pl.when(earlier & ~every)(lambda: add(team, key_block, True, True))
        pl.when((earlier & ~whole & every) | (key_block == least))(
            lambda: add(team, key_block, True, False)
        )
        return carry

    lax.fori_loop(0, held.shape[0] // TEAM, one_team, 0)
    for i in range(TEAM):
        at = i * rows
        upper = total[at : at + half] * inverse_ref[blocks[i] * tiles]
        lower = total[at + half : at + rows] * inverse_ref[blocks[i] * tiles + tiles - 1]
        packed = jnp.where(low, swap_halves(upper), lower)
        for more in before:
            packed = packed + more[i].astype(f32)
        out_ref[i] = packed.astype(out_ref.dtype)


def attend_call(tables, queries, keys, gives, *before):
    half, rows = queries.shape[1], 2 * queries.shape[1]
    steps = queries.shape[0] // TEAM
    packed = pl.BlockSpec((TEAM, half, LANES), lambda i, *_: (i, 0, 0))
    return pl.pallas_call(
        attend,
        grid_spec=pltpu.PrefetchScalarGridSpec(
            num_scalar_prefetch=5,
            grid=(steps,),
            in_specs=[
                packed,
                pl.BlockSpec(keys.shape, lambda i, *_: (0, 0, 0), pipeline_mode=pl.Buffered(1)),
            ]
            + [packed] * len(before),
            out_specs=packed,
            scratch_shapes=[
                pltpu.VMEM((TEAM * rows, LANES), f32),
                pltpu.VMEM((TEAM * rows, LANES), bf16),
            ],
        ),
        out_shape=jax.ShapeDtypeStruct(queries.shape, gives),
        compiler_params=pltpu.CompilerParams(vmem_limit_bytes=24 << 20),
        cost_estimate=pl.CostEstimate(
            flops=steps * 2_000_000_000, bytes_accessed=4_000_000, transcendentals=4_000_000
        ),
        name="attend",
    )(*tables, queries, keys, *before)


def finish(me_ref, tokens_ref, attention_ref, gating_ref, weights_ref, out_ref):
    rows = tokens_ref.shape[0]
    half = rows // 2
    low = low_lanes(half)
    uppers, lowers = [], []
    for pair in range(H // 2):
        one = attention_ref[jnp.bitwise_xor(me_ref[0], 2 * pair)].astype(f32)
        two = attention_ref[jnp.bitwise_xor(me_ref[0], 2 * pair + 1)].astype(f32)
        uppers.append(jnp.where(low, one, swap_halves(two)))
        lowers.append(jnp.where(low, swap_halves(one), two))
    attention = jnp.concatenate(
        [jnp.concatenate(uppers, axis=1), jnp.concatenate(lowers, axis=1)], axis=0
    )
    gated = (layer_norm(attention) * gating_ref[...].astype(f32)).astype(bf16)
    mixed = tokens_ref[...].astype(f32) + jnp.dot(
        gated, weights_ref[...], preferred_element_type=f32
    )
    out_ref[...] = mixed.astype(bf16)


VMEM = pl.BlockSpec(memory_space=pltpu.VMEM)
SMEM = pl.BlockSpec(memory_space=pltpu.SMEM)
HBM = pl.BlockSpec(memory_space=pltpu.HBM)


def per_device(seq_size, head_size, tokens, w_proj, w_out, tile_user):
    rows, width = tokens.shape
    half = rows // 2
    tiles = rows // TILE
    blocks = seq_size * head_size
    seq, head = lax.axis_index("seq"), lax.axis_index("head")
    fold = H // head_size
    share = fold
    groups = seq_size // (fold * share)
    group, part, core = seq // (fold * share), (seq // share) % fold, seq % share
    me = part * head_size + head
    me_array = me.reshape(1).astype(jnp.int32)

    def partner(array, k):
        if k == 0:
            return array
        pairs = []
        for s in range(seq_size):
            for h in range(head_size):
                g, p, c = s // (fold * share), (s // share) % fold, s % share
                other = (p * head_size + h) ^ k
                t = (g * fold + other // head_size) * share + c
                pairs.append((s * head_size + h, t * head_size + other % head_size))
        return lax.ppermute(array, ("seq", "head"), pairs)

    def seq_flip(array, bit):
        return lax.ppermute(array, "seq", [(s, s ^ bit) for s in range(seq_size)])

    sent = pl.pallas_call(
        project,
        out_shape=[jax.ShapeDtypeStruct((rows + half, LANES), bf16)] * H,
        in_specs=[SMEM, HBM, HBM],
        out_specs=[VMEM] * H,
        scratch_shapes=[
            pltpu.VMEM((rows, width), bf16),
            pltpu.VMEM((3, width, H * DH), bf16),
            pltpu.VMEM((H, rows + half, LANES), bf16),
            pltpu.SemaphoreType.DMA((4,)),
        ],
        compiler_params=pltpu.CompilerParams(vmem_limit_bytes=58 << 20),
        name="project",
    )(me_array, tokens, w_proj)
    def gating_of(tokens):
        return pl.pallas_call(
            project_gating,
            out_shape=jax.ShapeDtypeStruct((rows, H * DH), bf16),
            in_specs=[HBM, HBM],
            out_specs=VMEM,
            scratch_shapes=[
                pltpu.VMEM((rows, width), bf16),
                pltpu.VMEM((width, H * DH), bf16),
                pltpu.SemaphoreType.DMA((2,)),
            ],
            compiler_params=pltpu.CompilerParams(vmem_limit_bytes=12 << 20),
            name="project_gating",
        )(tokens, w_proj)

    start = jnp.sum((tile_user[None, :] < tile_user[:, None]).astype(jnp.int32), axis=1)
    length = jnp.sum((tile_user[None, :] == tile_user[:, None]).astype(f32), axis=1) * TILE
    asked = jnp.arange(H, dtype=jnp.int32) ^ me

    def blocks_of(places, in_group, in_core):
        in_seq = (in_group * fold + places // head_size) * share + in_core
        return in_seq * head_size + places % head_size

    def exchange(near, far):
        got = [(near[0], far[0])]
        for k in range(1, TEAM):
            both = partner(jnp.stack([near[k], far[k]]), k)
            got.append((both[0], both[1]))
        return jnp.stack([pair[0] for pair in got] + [pair[1] for pair in got])

    order = [0, 1, 5, 4, 2, 3, 6, 7]
    place_of = jnp.array([order.index(k) for k in range(H)], jnp.int32)
    arrived = {0: sent[0]}
    for k in order[1:-2]:
        arrived[k] = partner(sent[k], k)
    first_lot = jnp.stack([arrived[k][:rows] for k in order[:TEAM]])
    *held_back, first_lot = lax.optimization_barrier((sent[order[-2]], sent[order[-1]], first_lot))
    for k, array in zip(order[-2:], held_back):
        arrived[k] = partner(array, k)
    queries = jnp.stack([arrived[k][rows:] for k in range(H)])
    lots = [first_lot, jnp.stack([arrived[k][:rows] for k in order[TEAM:]])]
    keys = jnp.concatenate(lots)
    first_places = jnp.arange(0, H, TEAM, dtype=jnp.int32)
    mine = blocks_of(asked, group, core)
    if groups == 2 and share == 2:
        far_keys = jnp.concatenate([seq_flip(lot, fold * share) for lot in lots])
        other_queries = seq_flip(queries, 1)
        others = blocks_of(asked, group, 1 - core)

        def tables(query_blocks, in_group):
            teams = blocks_of(first_places, in_group, core)
            return start, 1.0 / length, query_blocks, teams, place_of[asked]

        near_ours = attend_call(tables(mine, group), queries, keys, f32)
        near_theirs = attend_call(tables(others, group), other_queries, keys, f32)
        gating = gating_of(lax.optimization_barrier((tokens, near_theirs))[0])
        far_keys, near_theirs, near_ours, gating = lax.optimization_barrier(
            (far_keys, near_theirs, near_ours, gating)
        )
        theirs = attend_call(
            tables(others, 1 - group), other_queries, far_keys, bf16, near_theirs
        )
        theirs = seq_flip(theirs, 1)
        team_b = attend_call(
            tables(mine[TEAM:], 1 - group), queries[TEAM:], far_keys, f32, near_ours[TEAM:]
        )
        attention_b = (team_b + theirs[TEAM:].astype(f32)).astype(bf16)
        attention_b, near_a = lax.optimization_barrier((attention_b, near_ours[:TEAM]))
        attention_a = attend_call(
            tables(mine[:TEAM], 1 - group), queries[:TEAM], far_keys, bf16, near_a, theirs[:TEAM]
        )
    else:
        everything = lax.all_gather(keys, "seq", axis=0, tiled=True)
        index = jnp.arange(blocks, dtype=jnp.int32)
        slot = index // head_size * H + place_of[jnp.bitwise_xor(index % head_size, me)]
        tables = (start, 1.0 / length, mine, index[::TEAM], slot)
        attention = attend_call(tables, queries, everything, bf16)
        attention_a, attention_b = attention[:TEAM], attention[TEAM:]
        gating = gating_of(tokens)
    returned = exchange(attention_a, partner(attention_b, TEAM))
    return pl.pallas_call(
        finish,
        out_shape=jax.ShapeDtypeStruct((rows, width), bf16),
        in_specs=[SMEM, VMEM, VMEM, VMEM, VMEM],
        out_specs=VMEM,
        compiler_params=pltpu.CompilerParams(vmem_limit_bytes=12 << 20),
        name="finish",
    )(me_array, tokens, returned, gating, w_out)


def solution(mesh):
    placed = (P(("seq", "head"), None), P(), P(), P())
    return jax.shard_map(
        functools.partial(per_device, mesh.shape["seq"], mesh.shape["head"]),
        mesh=mesh,
        in_specs=placed,
        out_specs=P(("seq", "head"), None),
        check_vma=False,
    )
```

```python
import functools

import jax
import jax.numpy as jnp
from jax import lax
from jax.experimental import pallas as pl
from jax.experimental.pallas import tpu as pltpu
from jax.sharding import PartitionSpec as P

H = 8
DH = 64
TILE = 128
LANES = 2 * DH
TEAM = H // 2

epsilon = 1e-05

f32 = jnp.float32
bf16 = jnp.bfloat16


def layer_norm(values):
    center = values - jnp.mean(values, axis=-1, keepdims=True)
    spread = jnp.mean(center * center, axis=-1, keepdims=True)
    return center * lax.rsqrt(spread + epsilon)


def silu(values):
    half = values * 0.5
    return half + half * jnp.tanh(half)


def swap_halves(values):
    return pltpu.roll(values, DH, 1)


def low_lanes(rows):
    return lax.broadcasted_iota(jnp.int32, (rows, LANES), 1) < DH


def project(me_ref, tokens_ref, weights_ref, *refs):
    outs, (tokens, weights, held, sems) = refs[:-4], refs[-4:]
    rows = tokens.shape[0]
    half = rows // 2
    copies = [[pltpu.make_async_copy(tokens_ref, tokens, sems.at[0])]]
    deep = weights.shape[1] // 2
    for i, block in enumerate((3, 1, 2)):
        pieces = []
        for j in range(2):
            inner = pl.ds(j * deep, deep)
            source = weights_ref.at[inner, pl.ds(block * H * DH, H * DH)]
            pieces.append(
                pltpu.make_async_copy(source, weights.at[i, inner], sems.at[1 + 2 * i + j])
            )
        copies.append(pieces)
    for pieces in copies:
        for copy in pieces:
            copy.start()

    def wait(number):
        for copy in copies[number]:
            copy.wait()

    wait(0)
    normed = layer_norm(tokens[...].astype(f32)).astype(bf16)
    low, half_low = low_lanes(rows), low_lanes(half)
    scale = 0.5 * DH ** (-0.5)
    wait(1)
    keys = silu(jnp.dot(normed, weights[0], preferred_element_type=f32))
    wait(2)
    values = silu(jnp.dot(normed, weights[1], preferred_element_type=f32))
    wait(3)
    queries = silu(jnp.dot(normed, weights[2], preferred_element_type=f32)) * scale
    for pair in range(H // 2):
        at = slice(pair * LANES, (pair + 1) * LANES)
        key, value, upper, lower = keys[:, at], values[:, at], queries[:half, at], queries[half:, at]
        held[2 * pair, :rows] = jnp.where(low, key, swap_halves(value)).astype(bf16)
        held[2 * pair + 1, :rows] = jnp.where(low, swap_halves(key), value).astype(bf16)
        held[2 * pair, rows:] = jnp.where(half_low, upper, swap_halves(lower)).astype(bf16)
        held[2 * pair + 1, rows:] = jnp.where(half_low, swap_halves(upper), lower).astype(bf16)
    for k, out in enumerate(outs):
        out[...] = held[jnp.bitwise_xor(me_ref[0], k)]


def project_gating(tokens_ref, weights_ref, out_ref, tokens, weights, sems):
    copies = [
        pltpu.make_async_copy(tokens_ref, tokens, sems.at[0]),
        pltpu.make_async_copy(weights_ref.at[:, pl.ds(0, H * DH)], weights, sems.at[1]),
    ]
    for copy in copies:
        copy.start()
    for copy in copies:
        copy.wait()
    normed = layer_norm(tokens[...].astype(f32)).astype(bf16)
    gating = silu(jnp.dot(normed, weights[...], preferred_element_type=f32))
    out_ref[...] = gating.astype(bf16)


def attend(
    start_ref, inverse_ref, block_ref, team_ref, slot_ref, queries_ref, held, *refs
):
    step = pl.program_id(0)
    *before, out_ref, total, queries = refs
    rows = held.shape[1]
    half = rows // 2
    tiles = rows // TILE
    low = low_lanes(half)
    blocks = [block_ref[step * TEAM + i] for i in range(TEAM)]
    for i in range(TEAM):
        packed = queries_ref[i].astype(f32)
        queries[i * rows : i * rows + half] = jnp.where(low, packed, 0.0).astype(bf16)
        queries[i * rows + half : (i + 1) * rows] = jnp.where(
            low, swap_halves(packed), 0.0
        ).astype(bf16)
    starts = [start_ref[block * tiles + j] for block in blocks for j in range(tiles)]
    least, low_start, high_start, high_first = blocks[0], starts[0], starts[0], starts[0]
    for block in blocks[1:]:
        least = jnp.minimum(least, block)
    for start in starts[1:]:
        low_start = jnp.minimum(low_start, start)
        high_start = jnp.maximum(high_start, start)
    for start in starts[tiles::tiles]:
        high_first = jnp.maximum(high_first, start)
    total[...] = jnp.zeros_like(total)

    def add(team, key_block, masked, chosen):
        key_rows = jnp.concatenate([held[slot_ref[team * TEAM + i]] for i in range(TEAM)], axis=0)
        if masked:
            column = lax.broadcasted_iota(jnp.int32, (TILE, TEAM * rows), 1)
            ahead = column - lax.broadcasted_iota(jnp.int32, (TILE, TEAM * rows), 0)

        def add_to(i):
            at = slice(i * rows, (i + 1) * rows)
            score = lax.dot_general(
                queries[at], key_rows, (((1,), (1,)), ((), ())), preferred_element_type=f32
            )
            weights = score + score * jnp.tanh(score)
            if masked:
                pieces = []
                for j in range(tiles):
                    from_start = starts[i * tiles + j] * TILE - key_block * rows
                    to_row = (blocks[i] - key_block) * rows + j * TILE
                    allowed = (column >= from_start) & (ahead <= to_row)
                    pieces.append(jnp.where(allowed, weights[j * TILE : (j + 1) * TILE], 0.0))
                weights = jnp.concatenate(pieces, axis=0)
            total[at] += jnp.dot(weights.astype(bf16), key_rows, preferred_element_type=f32)

        for i in range(TEAM):
            if chosen:
                needed = starts[i * tiles] < (key_block + TEAM) * tiles
                pl.when(needed)(functools.partial(add_to, i))
            else:
                add_to(i)

    def add_diagonal(team):
        key_rows = jnp.concatenate([held[slot_ref[team * TEAM + i]] for i in range(TEAM)], axis=0)
        turn = blocks[0] - least
        for i in range(TEAM):
            seen = (i + 1) * rows
            at = pl.ds(pl.multiple_of(jnp.bitwise_xor(turn, i) * rows, rows), rows)
            score = lax.dot_general(
                queries[at], key_rows[:seen], (((1,), (1,)), ((), ())), preferred_element_type=f32
            )
            weights = score + score * jnp.tanh(score)
            column = lax.broadcasted_iota(jnp.int32, (TILE, seen), 1)
            ahead = column - lax.broadcasted_iota(jnp.int32, (TILE, seen), 0)
            pieces = []
            for j in range(tiles):
                from_start = start_ref[(least + i) * tiles + j] * TILE - least * rows
                allowed = (column >= from_start) & (ahead <= i * rows + j * TILE)
                pieces.append(jnp.where(allowed, weights[j * TILE : (j + 1) * TILE], 0.0))
            weights = jnp.concatenate(pieces, axis=0).astype(bf16)
            total[at] += jnp.dot(weights, key_rows[:seen], preferred_element_type=f32)

    def one_team(team, carry):
        key_block = team_ref[team]
        earlier = (key_block < least) & ((key_block + TEAM) * tiles > low_start)
        whole = key_block * tiles >= high_start
        every = (key_block + TEAM) * tiles > high_first
        pl.when(earlier & whole)(lambda: add(team, key_block, False, False))
        pl.when(earlier & ~every)(lambda: add(team, key_block, True, True))
        pl.when(earlier & ~whole & every)(lambda: add(team, key_block, True, False))
        pl.when(key_block == least)(lambda: add_diagonal(team))
        return carry

    lax.fori_loop(0, held.shape[0] // TEAM, one_team, 0)
    for i in range(TEAM):
        at = i * rows
        upper = total[at : at + half] * inverse_ref[blocks[i] * tiles]
        lower = total[at + half : at + rows] * inverse_ref[blocks[i] * tiles + tiles - 1]
        packed = jnp.where(low, swap_halves(upper), lower)
        for more in before:
            packed = packed + more[i].astype(f32)
        out_ref[i] = packed.astype(out_ref.dtype)


def attend_call(tables, queries, keys, gives, *before):
    half, rows = queries.shape[1], 2 * queries.shape[1]
    steps = queries.shape[0] // TEAM
    packed = pl.BlockSpec((TEAM, half, LANES), lambda i, *_: (i, 0, 0))
    return pl.pallas_call(
        attend,
        grid_spec=pltpu.PrefetchScalarGridSpec(
            num_scalar_prefetch=5,
            grid=(steps,),
            in_specs=[
                packed,
                pl.BlockSpec(keys.shape, lambda i, *_: (0, 0, 0), pipeline_mode=pl.Buffered(1)),
            ]
            + [packed] * len(before),
            out_specs=packed,
            scratch_shapes=[
                pltpu.VMEM((TEAM * rows, LANES), f32),
                pltpu.VMEM((TEAM * rows, LANES), bf16),
            ],
        ),
        out_shape=jax.ShapeDtypeStruct(queries.shape, gives),
        compiler_params=pltpu.CompilerParams(vmem_limit_bytes=24 << 20),
        cost_estimate=pl.CostEstimate(
            flops=steps * 2_000_000_000, bytes_accessed=4_000_000, transcendentals=4_000_000
        ),
        name="attend",
    )(*tables, queries, keys, *before)


def finish(me_ref, tokens_ref, attention_ref, gating_ref, weights_ref, out_ref):
    rows = tokens_ref.shape[0]
    half = rows // 2
    low = low_lanes(half)
    uppers, lowers = [], []
    for pair in range(H // 2):
        one = attention_ref[jnp.bitwise_xor(me_ref[0], 2 * pair)].astype(f32)
        two = attention_ref[jnp.bitwise_xor(me_ref[0], 2 * pair + 1)].astype(f32)
        uppers.append(jnp.where(low, one, swap_halves(two)))
        lowers.append(jnp.where(low, swap_halves(one), two))
    attention = jnp.concatenate(
        [jnp.concatenate(uppers, axis=1), jnp.concatenate(lowers, axis=1)], axis=0
    )
    gated = (layer_norm(attention) * gating_ref[...].astype(f32)).astype(bf16)
    mixed = tokens_ref[...].astype(f32) + jnp.dot(
        gated, weights_ref[...], preferred_element_type=f32
    )
    out_ref[...] = mixed.astype(bf16)


VMEM = pl.BlockSpec(memory_space=pltpu.VMEM)
SMEM = pl.BlockSpec(memory_space=pltpu.SMEM)
HBM = pl.BlockSpec(memory_space=pltpu.HBM)


def per_device(seq_size, head_size, tokens, w_proj, w_out, tile_user):
    rows, width = tokens.shape
    half = rows // 2
    tiles = rows // TILE
    blocks = seq_size * head_size
    seq, head = lax.axis_index("seq"), lax.axis_index("head")
    fold = H // head_size
    share = fold
    groups = seq_size // (fold * share)
    group, part, core = seq // (fold * share), (seq // share) % fold, seq % share
    me = part * head_size + head
    me_array = me.reshape(1).astype(jnp.int32)

    def partner(array, k):
        if k == 0:
            return array
        pairs = []
        for s in range(seq_size):
            for h in range(head_size):
                g, p, c = s // (fold * share), (s // share) % fold, s % share
                other = (p * head_size + h) ^ k
                t = (g * fold + other // head_size) * share + c
                pairs.append((s * head_size + h, t * head_size + other % head_size))
        return lax.ppermute(array, ("seq", "head"), pairs)

    def seq_flip(array, bit):
        return lax.ppermute(array, "seq", [(s, s ^ bit) for s in range(seq_size)])

    sent = pl.pallas_call(
        project,
        out_shape=[jax.ShapeDtypeStruct((rows + half, LANES), bf16)] * H,
        in_specs=[SMEM, HBM, HBM],
        out_specs=[VMEM] * H,
        scratch_shapes=[
            pltpu.VMEM((rows, width), bf16),
            pltpu.VMEM((3, width, H * DH), bf16),
            pltpu.VMEM((H, rows + half, LANES), bf16),
            pltpu.SemaphoreType.DMA((7,)),
        ],
        compiler_params=pltpu.CompilerParams(vmem_limit_bytes=52 << 20),
        name="project",
    )(me_array, tokens, w_proj)
    def gating_of(tokens):
        return pl.pallas_call(
            project_gating,
            out_shape=jax.ShapeDtypeStruct((rows, H * DH), bf16),
            in_specs=[HBM, HBM],
            out_specs=VMEM,
            scratch_shapes=[
                pltpu.VMEM((rows, width), bf16),
                pltpu.VMEM((width, H * DH), bf16),
                pltpu.SemaphoreType.DMA((2,)),
            ],
            compiler_params=pltpu.CompilerParams(vmem_limit_bytes=12 << 20),
            name="project_gating",
        )(tokens, w_proj)

    start = jnp.sum((tile_user[None, :] < tile_user[:, None]).astype(jnp.int32), axis=1)
    length = jnp.sum((tile_user[None, :] == tile_user[:, None]).astype(f32), axis=1) * TILE
    asked = jnp.arange(H, dtype=jnp.int32) ^ me

    def blocks_of(places, in_group, in_core):
        in_seq = (in_group * fold + places // head_size) * share + in_core
        return in_seq * head_size + places % head_size

    def exchange(near, far):
        got = [(near[0], far[0])]
        for k in range(1, TEAM):
            both = partner(jnp.stack([near[k], far[k]]), k)
            got.append((both[0], both[1]))
        return jnp.stack([pair[0] for pair in got] + [pair[1] for pair in got])

    order = [0, 1, 5, 4, 2, 3, 6, 7]
    place_of = jnp.array([order.index(k) for k in range(H)], jnp.int32)
    arrived = {0: sent[0]}
    for k in order[1:-2]:
        arrived[k] = partner(sent[k], k)
    nearest = order[1:3]
    *held_back, arrived[nearest[0]], arrived[nearest[1]] = lax.optimization_barrier(
        (sent[order[-2]], sent[order[-1]], arrived[nearest[0]], arrived[nearest[1]])
    )
    for k, array in zip(order[-2:], held_back):
        arrived[k] = partner(array, k)
    first_lot = jnp.stack([arrived[k][:rows] for k in order[:TEAM]])
    queries = jnp.stack([arrived[k][rows:] for k in range(H)])
    lots = [first_lot, jnp.stack([arrived[k][:rows] for k in order[TEAM:]])]
    keys = jnp.concatenate(lots)
    first_places = jnp.arange(0, H, TEAM, dtype=jnp.int32)
    mine = blocks_of(asked, group, core)
    if groups == 2 and share == 2:
        far_keys = jnp.concatenate([seq_flip(lot, fold * share) for lot in lots])
        other_queries = seq_flip(queries, 1)
        others = blocks_of(asked, group, 1 - core)

        def tables(query_blocks, in_group):
            teams = blocks_of(first_places, in_group, core)
            return start, 1.0 / length, query_blocks, teams, place_of[asked]

        near_ours = attend_call(tables(mine, group), queries, keys, f32)
        near_theirs = attend_call(tables(others, group), other_queries, keys, f32)
        gating = gating_of(lax.optimization_barrier((tokens, near_theirs))[0])
        far_keys, near_theirs, near_ours, gating = lax.optimization_barrier(
            (far_keys, near_theirs, near_ours, gating)
        )
        theirs = attend_call(
            tables(others, 1 - group), other_queries, far_keys, bf16, near_theirs
        )
        theirs = seq_flip(theirs, 1)
        team_b = attend_call(
            tables(mine[TEAM:], 1 - group), queries[TEAM:], far_keys, f32, near_ours[TEAM:]
        )
        attention_b = (team_b + theirs[TEAM:].astype(f32)).astype(bf16)
        attention_b, near_a = lax.optimization_barrier((attention_b, near_ours[:TEAM]))
        attention_a = attend_call(
            tables(mine[:TEAM], 1 - group), queries[:TEAM], far_keys, bf16, near_a, theirs[:TEAM]
        )
    else:
        everything = lax.all_gather(keys, "seq", axis=0, tiled=True)
        index = jnp.arange(blocks, dtype=jnp.int32)
        slot = index // head_size * H + place_of[jnp.bitwise_xor(index % head_size, me)]
        tables = (start, 1.0 / length, mine, index[::TEAM], slot)
        attention = attend_call(tables, queries, everything, bf16)
        attention_a, attention_b = attention[:TEAM], attention[TEAM:]
        gating = gating_of(tokens)
    returned = exchange(attention_a, partner(attention_b, TEAM))
    return pl.pallas_call(
        finish,
        out_shape=jax.ShapeDtypeStruct((rows, width), bf16),
        in_specs=[SMEM, VMEM, VMEM, VMEM, VMEM],
        out_specs=VMEM,
        compiler_params=pltpu.CompilerParams(vmem_limit_bytes=12 << 20),
        name="finish",
    )(me_array, tokens, returned, gating, w_out)


def solution(mesh):
    placed = (P(("seq", "head"), None), P(), P(), P())
    return jax.shard_map(
        functools.partial(per_device, mesh.shape["seq"], mesh.shape["head"]),
        mesh=mesh,
        in_specs=placed,
        out_specs=P(("seq", "head"), None),
        check_vma=False,
    )
```

```python
import functools

import jax
import jax.numpy as jnp
from jax import lax
from jax.experimental import pallas as pl
from jax.experimental.pallas import tpu as pltpu
from jax.sharding import PartitionSpec as P

H = 8
DH = 64
TILE = 128
LANES = 2 * DH
TEAM = H // 2

epsilon = 1e-05

f32 = jnp.float32
bf16 = jnp.bfloat16


def layer_norm(values):
    center = values - jnp.mean(values, axis=-1, keepdims=True)
    spread = jnp.mean(center * center, axis=-1, keepdims=True)
    return center * lax.rsqrt(spread + epsilon)


def silu(values):
    half = values * 0.5
    return half + half * jnp.tanh(half)


def swap_halves(values):
    return pltpu.roll(values, DH, 1)


def low_lanes(rows):
    return lax.broadcasted_iota(jnp.int32, (rows, LANES), 1) < DH


def project(me_ref, tokens_ref, weights_ref, *refs):
    outs, (tokens, weights, held, sems) = refs[:-4], refs[-4:]
    rows = tokens.shape[0]
    half = rows // 2
    copies = [[pltpu.make_async_copy(tokens_ref, tokens, sems.at[0])]]
    deep = weights.shape[1] // 2
    for i, block in enumerate((3, 1, 2)):
        pieces = []
        for j in range(2):
            inner = pl.ds(j * deep, deep)
            source = weights_ref.at[inner, pl.ds(block * H * DH, H * DH)]
            pieces.append(
                pltpu.make_async_copy(source, weights.at[i, inner], sems.at[1 + 2 * i + j])
            )
        copies.append(pieces)
    for pieces in copies:
        for copy in pieces:
            copy.start()

    def wait(number):
        for copy in copies[number]:
            copy.wait()

    wait(0)
    normed = layer_norm(tokens[...].astype(f32)).astype(bf16)
    low, half_low = low_lanes(rows), low_lanes(half)
    scale = 0.5 * DH ** (-0.5)
    wait(1)
    keys = silu(jnp.dot(normed, weights[0], preferred_element_type=f32))
    wait(2)
    values = silu(jnp.dot(normed, weights[1], preferred_element_type=f32))
    for pair in range(H // 2):
        at = slice(pair * LANES, (pair + 1) * LANES)
        key, value = keys[:, at], values[:, at]
        held[2 * pair, :rows] = jnp.where(low, key, swap_halves(value)).astype(bf16)
        held[2 * pair + 1, :rows] = jnp.where(low, swap_halves(key), value).astype(bf16)
    wait(3)
    queries = silu(jnp.dot(normed, weights[2], preferred_element_type=f32)) * scale
    for pair in range(H // 2):
        at = slice(pair * LANES, (pair + 1) * LANES)
        upper, lower = queries[:half, at], queries[half:, at]
        held[2 * pair, rows:] = jnp.where(half_low, upper, swap_halves(lower)).astype(bf16)
        held[2 * pair + 1, rows:] = jnp.where(half_low, swap_halves(upper), lower).astype(bf16)
    for k, out in enumerate(outs):
        out[...] = held[jnp.bitwise_xor(me_ref[0], k)]


def project_gating(tokens_ref, weights_ref, out_ref, tokens, weights, sems):
    copies = [
        pltpu.make_async_copy(tokens_ref, tokens, sems.at[0]),
        pltpu.make_async_copy(weights_ref.at[:, pl.ds(0, H * DH)], weights, sems.at[1]),
    ]
    for copy in copies:
        copy.start()
    for copy in copies:
        copy.wait()
    normed = layer_norm(tokens[...].astype(f32)).astype(bf16)
    gating = silu(jnp.dot(normed, weights[...], preferred_element_type=f32))
    out_ref[...] = gating.astype(bf16)


def attend(
    start_ref, inverse_ref, block_ref, team_ref, slot_ref, queries_ref, held, *refs
):
    step = pl.program_id(0)
    *before, out_ref, total, queries = refs
    rows = held.shape[1]
    half = rows // 2
    tiles = rows // TILE
    low = low_lanes(half)
    blocks = [block_ref[step * TEAM + i] for i in range(TEAM)]
    for i in range(TEAM):
        packed = queries_ref[i].astype(f32)
        queries[i * rows : i * rows + half] = jnp.where(low, packed, 0.0).astype(bf16)
        queries[i * rows + half : (i + 1) * rows] = jnp.where(
            low, swap_halves(packed), 0.0
        ).astype(bf16)
    starts = [start_ref[block * tiles + j] for block in blocks for j in range(tiles)]
    least, low_start, high_start, high_first = blocks[0], starts[0], starts[0], starts[0]
    for block in blocks[1:]:
        least = jnp.minimum(least, block)
    for start in starts[1:]:
        low_start = jnp.minimum(low_start, start)
        high_start = jnp.maximum(high_start, start)
    for start in starts[tiles::tiles]:
        high_first = jnp.maximum(high_first, start)
    total[...] = jnp.zeros_like(total)

    def add(team, key_block, masked, chosen):
        key_rows = jnp.concatenate([held[slot_ref[team * TEAM + i]] for i in range(TEAM)], axis=0)
        if masked:
            column = lax.broadcasted_iota(jnp.int32, (TILE, TEAM * rows), 1)
            ahead = column - lax.broadcasted_iota(jnp.int32, (TILE, TEAM * rows), 0)

        def add_to(i):
            at = slice(i * rows, (i + 1) * rows)
            score = lax.dot_general(
                queries[at], key_rows, (((1,), (1,)), ((), ())), preferred_element_type=f32
            )
            weights = score + score * jnp.tanh(score)
            if masked:
                pieces = []
                for j in range(tiles):
                    from_start = starts[i * tiles + j] * TILE - key_block * rows
                    to_row = (blocks[i] - key_block) * rows + j * TILE
                    allowed = (column >= from_start) & (ahead <= to_row)
                    pieces.append(jnp.where(allowed, weights[j * TILE : (j + 1) * TILE], 0.0))
                weights = jnp.concatenate(pieces, axis=0)
            total[at] += jnp.dot(weights.astype(bf16), key_rows, preferred_element_type=f32)

        for i in range(TEAM):
            if chosen:
                needed = starts[i * tiles] < (key_block + TEAM) * tiles
                pl.when(needed)(functools.partial(add_to, i))
            else:
                add_to(i)

    def add_diagonal(team):
        key_rows = jnp.concatenate([held[slot_ref[team * TEAM + i]] for i in range(TEAM)], axis=0)
        turn = blocks[0] - least
        for i in range(TEAM):
            seen = (i + 1) * rows
            at = pl.ds(pl.multiple_of(jnp.bitwise_xor(turn, i) * rows, rows), rows)
            score = lax.dot_general(
                queries[at], key_rows[:seen], (((1,), (1,)), ((), ())), preferred_element_type=f32
            )
            weights = score + score * jnp.tanh(score)
            column = lax.broadcasted_iota(jnp.int32, (TILE, seen), 1)
            ahead = column - lax.broadcasted_iota(jnp.int32, (TILE, seen), 0)
            pieces = []
            for j in range(tiles):
                from_start = start_ref[(least + i) * tiles + j] * TILE - least * rows
                allowed = (column >= from_start) & (ahead <= i * rows + j * TILE)
                pieces.append(jnp.where(allowed, weights[j * TILE : (j + 1) * TILE], 0.0))
            weights = jnp.concatenate(pieces, axis=0).astype(bf16)
            total[at] += jnp.dot(weights, key_rows[:seen], preferred_element_type=f32)

    def one_team(team, carry):
        key_block = team_ref[team]
        earlier = (key_block < least) & ((key_block + TEAM) * tiles > low_start)
        whole = key_block * tiles >= high_start
        every = (key_block + TEAM) * tiles > high_first
        pl.when(earlier & whole)(lambda: add(team, key_block, False, False))
        pl.when(earlier & ~every)(lambda: add(team, key_block, True, True))
        pl.when(earlier & ~whole & every)(lambda: add(team, key_block, True, False))
        pl.when(key_block == least)(lambda: add_diagonal(team))
        return carry

    lax.fori_loop(0, held.shape[0] // TEAM, one_team, 0)
    for i in range(TEAM):
        at = i * rows
        upper = total[at : at + half] * inverse_ref[blocks[i] * tiles]
        lower = total[at + half : at + rows] * inverse_ref[blocks[i] * tiles + tiles - 1]
        packed = jnp.where(low, swap_halves(upper), lower)
        for more in before:
            packed = packed + more[i].astype(f32)
        out_ref[i] = packed.astype(out_ref.dtype)


def attend_call(tables, queries, keys, gives, *before):
    half, rows = queries.shape[1], 2 * queries.shape[1]
    steps = queries.shape[0] // TEAM
    packed = pl.BlockSpec((TEAM, half, LANES), lambda i, *_: (i, 0, 0))
    return pl.pallas_call(
        attend,
        grid_spec=pltpu.PrefetchScalarGridSpec(
            num_scalar_prefetch=5,
            grid=(steps,),
            in_specs=[
                packed,
                pl.BlockSpec(keys.shape, lambda i, *_: (0, 0, 0), pipeline_mode=pl.Buffered(1)),
            ]
            + [packed] * len(before),
            out_specs=packed,
            scratch_shapes=[
                pltpu.VMEM((TEAM * rows, LANES), f32),
                pltpu.VMEM((TEAM * rows, LANES), bf16),
            ],
        ),
        out_shape=jax.ShapeDtypeStruct(queries.shape, gives),
        compiler_params=pltpu.CompilerParams(vmem_limit_bytes=24 << 20),
        cost_estimate=pl.CostEstimate(
            flops=steps * 2_000_000_000, bytes_accessed=4_000_000, transcendentals=4_000_000
        ),
        name="attend",
    )(*tables, queries, keys, *before)


def finish(me_ref, tokens_ref, attention_ref, gating_ref, weights_ref, out_ref):
    rows = tokens_ref.shape[0]
    half = rows // 2
    low = low_lanes(half)
    uppers, lowers = [], []
    for pair in range(H // 2):
        one = attention_ref[jnp.bitwise_xor(me_ref[0], 2 * pair)].astype(f32)
        two = attention_ref[jnp.bitwise_xor(me_ref[0], 2 * pair + 1)].astype(f32)
        uppers.append(jnp.where(low, one, swap_halves(two)))
        lowers.append(jnp.where(low, swap_halves(one), two))
    attention = jnp.concatenate(
        [jnp.concatenate(uppers, axis=1), jnp.concatenate(lowers, axis=1)], axis=0
    )
    gated = (layer_norm(attention) * gating_ref[...].astype(f32)).astype(bf16)
    mixed = tokens_ref[...].astype(f32) + jnp.dot(
        gated, weights_ref[...], preferred_element_type=f32
    )
    out_ref[...] = mixed.astype(bf16)


VMEM = pl.BlockSpec(memory_space=pltpu.VMEM)
SMEM = pl.BlockSpec(memory_space=pltpu.SMEM)
HBM = pl.BlockSpec(memory_space=pltpu.HBM)


def per_device(seq_size, head_size, tokens, w_proj, w_out, tile_user):
    rows, width = tokens.shape
    half = rows // 2
    tiles = rows // TILE
    blocks = seq_size * head_size
    seq, head = lax.axis_index("seq"), lax.axis_index("head")
    fold = H // head_size
    share = fold
    groups = seq_size // (fold * share)
    group, part, core = seq // (fold * share), (seq // share) % fold, seq % share
    me = part * head_size + head
    me_array = me.reshape(1).astype(jnp.int32)

    def partner(array, k):
        if k == 0:
            return array
        pairs = []
        for s in range(seq_size):
            for h in range(head_size):
                g, p, c = s // (fold * share), (s // share) % fold, s % share
                other = (p * head_size + h) ^ k
                t = (g * fold + other // head_size) * share + c
                pairs.append((s * head_size + h, t * head_size + other % head_size))
        return lax.ppermute(array, ("seq", "head"), pairs)

    def seq_flip(array, bit):
        return lax.ppermute(array, "seq", [(s, s ^ bit) for s in range(seq_size)])

    sent = pl.pallas_call(
        project,
        out_shape=[jax.ShapeDtypeStruct((rows + half, LANES), bf16)] * H,
        in_specs=[SMEM, HBM, HBM],
        out_specs=[VMEM] * H,
        scratch_shapes=[
            pltpu.VMEM((rows, width), bf16),
            pltpu.VMEM((3, width, H * DH), bf16),
            pltpu.VMEM((H, rows + half, LANES), bf16),
            pltpu.SemaphoreType.DMA((7,)),
        ],
        compiler_params=pltpu.CompilerParams(vmem_limit_bytes=53 << 20),
        name="project",
    )(me_array, tokens, w_proj)
    def gating_of(tokens):
        return pl.pallas_call(
            project_gating,
            out_shape=jax.ShapeDtypeStruct((rows, H * DH), bf16),
            in_specs=[HBM, HBM],
            out_specs=VMEM,
            scratch_shapes=[
                pltpu.VMEM((rows, width), bf16),
                pltpu.VMEM((width, H * DH), bf16),
                pltpu.SemaphoreType.DMA((2,)),
            ],
            compiler_params=pltpu.CompilerParams(vmem_limit_bytes=12 << 20),
            name="project_gating",
        )(tokens, w_proj)

    start = jnp.sum((tile_user[None, :] < tile_user[:, None]).astype(jnp.int32), axis=1)
    length = jnp.sum((tile_user[None, :] == tile_user[:, None]).astype(f32), axis=1) * TILE
    asked = jnp.arange(H, dtype=jnp.int32) ^ me

    def blocks_of(places, in_group, in_core):
        in_seq = (in_group * fold + places // head_size) * share + in_core
        return in_seq * head_size + places % head_size

    def exchange(near, far):
        got = [(near[0], far[0])]
        for k in range(1, TEAM):
            both = partner(jnp.stack([near[k], far[k]]), k)
            got.append((both[0], both[1]))
        return jnp.stack([pair[0] for pair in got] + [pair[1] for pair in got])

    order = [0, 1, 5, 4, 2, 3, 6, 7]
    place_of = jnp.array([order.index(k) for k in range(H)], jnp.int32)
    arrived = {0: sent[0]}
    for k in order[1:-2]:
        arrived[k] = partner(sent[k], k)
    first_lot = jnp.stack([arrived[k][:rows] for k in order[:TEAM]])
    *held_back, first_lot = lax.optimization_barrier((sent[order[-2]], sent[order[-1]], first_lot))
    for k, array in zip(order[-2:], held_back):
        arrived[k] = partner(array, k)
    queries = jnp.stack([arrived[k][rows:] for k in range(H)])
    lots = [first_lot, jnp.stack([arrived[k][:rows] for k in order[TEAM:]])]
    keys = jnp.concatenate(lots)
    first_places = jnp.arange(0, H, TEAM, dtype=jnp.int32)
    mine = blocks_of(asked, group, core)
    if groups == 2 and share == 2:
        far_keys = jnp.concatenate([seq_flip(lot, fold * share) for lot in lots])
        other_queries = seq_flip(queries, 1)
        others = blocks_of(asked, group, 1 - core)

        def tables(query_blocks, in_group):
            teams = blocks_of(first_places, in_group, core)
            return start, 1.0 / length, query_blocks, teams, place_of[asked]

        near_ours = attend_call(tables(mine, group), queries, keys, f32)
        near_theirs = attend_call(tables(others, group), other_queries, keys, f32)
        gating = gating_of(lax.optimization_barrier((tokens, near_theirs))[0])
        far_keys, near_theirs, near_ours, gating = lax.optimization_barrier(
            (far_keys, near_theirs, near_ours, gating)
        )
        theirs = attend_call(
            tables(others, 1 - group), other_queries, far_keys, bf16, near_theirs
        )
        theirs = seq_flip(theirs, 1)
        ours = attend_call(tables(mine, 1 - group), queries, far_keys, f32, near_ours)
        attention = (ours + theirs.astype(f32)).astype(bf16)
    else:
        everything = lax.all_gather(keys, "seq", axis=0, tiled=True)
        index = jnp.arange(blocks, dtype=jnp.int32)
        slot = index // head_size * H + place_of[jnp.bitwise_xor(index % head_size, me)]
        tables = (start, 1.0 / length, mine, index[::TEAM], slot)
        attention = attend_call(tables, queries, everything, bf16)
        gating = gating_of(tokens)
    returned = exchange(attention[:TEAM], partner(attention[TEAM:], TEAM))
    return pl.pallas_call(
        finish,
        out_shape=jax.ShapeDtypeStruct((rows, width), bf16),
        in_specs=[SMEM, VMEM, VMEM, VMEM, VMEM],
        out_specs=VMEM,
        compiler_params=pltpu.CompilerParams(vmem_limit_bytes=12 << 20),
        name="finish",
    )(me_array, tokens, returned, gating, w_out)


def solution(mesh):
    placed = (P(("seq", "head"), None), P(), P(), P())
    return jax.shard_map(
        functools.partial(per_device, mesh.shape["seq"], mesh.shape["head"]),
        mesh=mesh,
        in_specs=placed,
        out_specs=P(("seq", "head"), None),
        check_vma=False,
    )
```

```python
import functools

import jax
import jax.numpy as jnp
from jax import lax
from jax.experimental import pallas as pl
from jax.experimental.pallas import tpu as pltpu
from jax.sharding import PartitionSpec as P

H = 8
DH = 64
TILE = 128
LANES = 2 * DH
TEAM = H // 2

epsilon = 1e-05

f32 = jnp.float32
bf16 = jnp.bfloat16


def layer_norm(values):
    center = values - jnp.mean(values, axis=-1, keepdims=True)
    spread = jnp.mean(center * center, axis=-1, keepdims=True)
    return center * lax.rsqrt(spread + epsilon)


def silu(values):
    half = values * 0.5
    return half + half * jnp.tanh(half)


def swap_halves(values):
    return pltpu.roll(values, DH, 1)


def low_lanes(rows):
    return lax.broadcasted_iota(jnp.int32, (rows, LANES), 1) < DH


def project(me_ref, tokens_ref, weights_ref, *refs):
    outs, (tokens, weights, held, sems) = refs[:-4], refs[-4:]
    rows = tokens.shape[0]
    half = rows // 2
    copies = [[pltpu.make_async_copy(tokens_ref, tokens, sems.at[0])]]
    deep = weights.shape[1] // 2
    for i, block in enumerate((3, 1, 2)):
        pieces = []
        for j in range(2):
            inner = pl.ds(j * deep, deep)
            source = weights_ref.at[inner, pl.ds(block * H * DH, H * DH)]
            pieces.append(
                pltpu.make_async_copy(source, weights.at[i, inner], sems.at[1 + 2 * i + j])
            )
        copies.append(pieces)
    for pieces in copies:
        for copy in pieces:
            copy.start()

    def wait(number):
        for copy in copies[number]:
            copy.wait()

    wait(0)
    normed = layer_norm(tokens[...].astype(f32)).astype(bf16)
    low, half_low = low_lanes(rows), low_lanes(half)
    scale = 0.5 * DH ** (-0.5)
    wait(1)
    keys = silu(jnp.dot(normed, weights[0], preferred_element_type=f32))
    wait(2)
    values = silu(jnp.dot(normed, weights[1], preferred_element_type=f32))
    for pair in range(H // 2):
        at = slice(pair * LANES, (pair + 1) * LANES)
        key, value = keys[:, at], values[:, at]
        held[2 * pair, :rows] = jnp.where(low, key, swap_halves(value)).astype(bf16)
        held[2 * pair + 1, :rows] = jnp.where(low, swap_halves(key), value).astype(bf16)
    wait(3)
    queries = silu(jnp.dot(normed, weights[2], preferred_element_type=f32)) * scale
    for pair in range(H // 2):
        at = slice(pair * LANES, (pair + 1) * LANES)
        upper, lower = queries[:half, at], queries[half:, at]
        held[2 * pair, rows:] = jnp.where(half_low, upper, swap_halves(lower)).astype(bf16)
        held[2 * pair + 1, rows:] = jnp.where(half_low, swap_halves(upper), lower).astype(bf16)
    for k, out in enumerate(outs):
        out[...] = held[jnp.bitwise_xor(me_ref[0], k)]


def project_gating(tokens_ref, weights_ref, out_ref, tokens, weights, sems):
    copies = [
        pltpu.make_async_copy(tokens_ref, tokens, sems.at[0]),
        pltpu.make_async_copy(weights_ref.at[:, pl.ds(0, H * DH)], weights, sems.at[1]),
    ]
    for copy in copies:
        copy.start()
    for copy in copies:
        copy.wait()
    normed = layer_norm(tokens[...].astype(f32)).astype(bf16)
    gating = silu(jnp.dot(normed, weights[...], preferred_element_type=f32))
    out_ref[...] = gating.astype(bf16)


def attend(
    start_ref, inverse_ref, block_ref, team_ref, slot_ref, out_team, queries_ref, held, *refs
):
    step = pl.program_id(0)
    *before, out_ref, total, queries = refs
    rows = held.shape[1]
    half = rows // 2
    tiles = rows // TILE
    low = low_lanes(half)
    blocks = [block_ref[step * TEAM + i] for i in range(TEAM)]
    for i in range(TEAM):
        packed = queries_ref[i].astype(f32)
        queries[i * rows : i * rows + half] = jnp.where(low, packed, 0.0).astype(bf16)
        queries[i * rows + half : (i + 1) * rows] = jnp.where(
            low, swap_halves(packed), 0.0
        ).astype(bf16)
    starts = [start_ref[block * tiles + j] for block in blocks for j in range(tiles)]
    least, low_start, high_start, high_first = blocks[0], starts[0], starts[0], starts[0]
    for block in blocks[1:]:
        least = jnp.minimum(least, block)
    for start in starts[1:]:
        low_start = jnp.minimum(low_start, start)
        high_start = jnp.maximum(high_start, start)
    for start in starts[tiles::tiles]:
        high_first = jnp.maximum(high_first, start)
    total[...] = jnp.zeros_like(total)

    def add(team, key_block, masked, chosen):
        key_rows = jnp.concatenate([held[slot_ref[team * TEAM + i]] for i in range(TEAM)], axis=0)
        if masked:
            column = lax.broadcasted_iota(jnp.int32, (TILE, TEAM * rows), 1)
            ahead = column - lax.broadcasted_iota(jnp.int32, (TILE, TEAM * rows), 0)

        def add_to(i):
            at = slice(i * rows, (i + 1) * rows)
            score = lax.dot_general(
                queries[at], key_rows, (((1,), (1,)), ((), ())), preferred_element_type=f32
            )
            weights = score + score * jnp.tanh(score)
            if masked:
                pieces = []
                for j in range(tiles):
                    from_start = starts[i * tiles + j] * TILE - key_block * rows
                    to_row = (blocks[i] - key_block) * rows + j * TILE
                    allowed = (column >= from_start) & (ahead <= to_row)
                    pieces.append(jnp.where(allowed, weights[j * TILE : (j + 1) * TILE], 0.0))
                weights = jnp.concatenate(pieces, axis=0)
            total[at] += jnp.dot(weights.astype(bf16), key_rows, preferred_element_type=f32)

        for i in range(TEAM):
            if chosen:
                needed = starts[i * tiles] < (key_block + TEAM) * tiles
                pl.when(needed)(functools.partial(add_to, i))
            else:
                add_to(i)

    def add_diagonal(team):
        key_rows = jnp.concatenate([held[slot_ref[team * TEAM + i]] for i in range(TEAM)], axis=0)
        turn = blocks[0] - least
        for i in range(TEAM):
            seen = (i + 1) * rows
            at = pl.ds(pl.multiple_of(jnp.bitwise_xor(turn, i) * rows, rows), rows)
            score = lax.dot_general(
                queries[at], key_rows[:seen], (((1,), (1,)), ((), ())), preferred_element_type=f32
            )
            weights = score + score * jnp.tanh(score)
            column = lax.broadcasted_iota(jnp.int32, (TILE, seen), 1)
            ahead = column - lax.broadcasted_iota(jnp.int32, (TILE, seen), 0)
            pieces = []
            for j in range(tiles):
                from_start = start_ref[(least + i) * tiles + j] * TILE - least * rows
                allowed = (column >= from_start) & (ahead <= i * rows + j * TILE)
                pieces.append(jnp.where(allowed, weights[j * TILE : (j + 1) * TILE], 0.0))
            weights = jnp.concatenate(pieces, axis=0).astype(bf16)
            total[at] += jnp.dot(weights, key_rows[:seen], preferred_element_type=f32)

    def one_team(team, carry):
        key_block = team_ref[team]
        earlier = (key_block < least) & ((key_block + TEAM) * tiles > low_start)
        whole = key_block * tiles >= high_start
        every = (key_block + TEAM) * tiles > high_first
        pl.when(earlier & whole)(lambda: add(team, key_block, False, False))
        pl.when(earlier & ~every)(lambda: add(team, key_block, True, True))
        pl.when(earlier & ~whole & every)(lambda: add(team, key_block, True, False))
        pl.when(key_block == least)(lambda: add_diagonal(team))
        return carry

    lax.fori_loop(0, held.shape[0] // TEAM, one_team, 0)
    for i in range(TEAM):
        at = i * rows
        upper = total[at : at + half] * inverse_ref[blocks[i] * tiles]
        lower = total[at + half : at + rows] * inverse_ref[blocks[i] * tiles + tiles - 1]
        packed = jnp.where(low, swap_halves(upper), lower)
        for more in before:
            packed = packed + more[blocks[i] - least].astype(f32)
        out_ref[blocks[i] - least] = packed.astype(out_ref.dtype)


def attend_call(tables, queries, keys, gives, *before):
    half, rows = queries.shape[1], 2 * queries.shape[1]
    steps = queries.shape[0] // TEAM
    packed = pl.BlockSpec((TEAM, half, LANES), lambda i, *_: (i, 0, 0))
    placed = pl.BlockSpec((TEAM, half, LANES), lambda i, *refs: (refs[5][i], 0, 0))
    return pl.pallas_call(
        attend,
        grid_spec=pltpu.PrefetchScalarGridSpec(
            num_scalar_prefetch=6,
            grid=(steps,),
            in_specs=[
                packed,
                pl.BlockSpec(keys.shape, lambda i, *_: (0, 0, 0), pipeline_mode=pl.Buffered(1)),
            ]
            + [placed] * len(before),
            out_specs=placed,
            scratch_shapes=[
                pltpu.VMEM((TEAM * rows, LANES), f32),
                pltpu.VMEM((TEAM * rows, LANES), bf16),
            ],
        ),
        out_shape=jax.ShapeDtypeStruct(queries.shape, gives),
        compiler_params=pltpu.CompilerParams(vmem_limit_bytes=24 << 20),
        cost_estimate=pl.CostEstimate(
            flops=steps * 2_000_000_000, bytes_accessed=4_000_000, transcendentals=4_000_000
        ),
        name="attend",
    )(*tables, queries, keys, *before)


def finish(tokens_ref, attention_ref, gating_ref, weights_ref, out_ref):
    rows = tokens_ref.shape[0]
    half = rows // 2
    low = low_lanes(half)
    uppers, lowers = [], []
    for pair in range(H // 2):
        one = attention_ref[2 * pair].astype(f32)
        two = attention_ref[2 * pair + 1].astype(f32)
        uppers.append(jnp.where(low, one, swap_halves(two)))
        lowers.append(jnp.where(low, swap_halves(one), two))
    attention = jnp.concatenate(
        [jnp.concatenate(uppers, axis=1), jnp.concatenate(lowers, axis=1)], axis=0
    )
    gated = (layer_norm(attention) * gating_ref[...].astype(f32)).astype(bf16)
    mixed = tokens_ref[...].astype(f32) + jnp.dot(
        gated, weights_ref[...], preferred_element_type=f32
    )
    out_ref[...] = mixed.astype(bf16)


VMEM = pl.BlockSpec(memory_space=pltpu.VMEM)
SMEM = pl.BlockSpec(memory_space=pltpu.SMEM)
HBM = pl.BlockSpec(memory_space=pltpu.HBM)


def per_device(seq_size, head_size, tokens, w_proj, w_out, tile_user):
    rows, width = tokens.shape
    half = rows // 2
    tiles = rows // TILE
    blocks = seq_size * head_size
    seq, head = lax.axis_index("seq"), lax.axis_index("head")
    fold = H // head_size
    share = fold
    groups = seq_size // (fold * share)
    group, part, core = seq // (fold * share), (seq // share) % fold, seq % share
    me = part * head_size + head
    me_array = me.reshape(1).astype(jnp.int32)

    def partner(array, k):
        if k == 0:
            return array
        pairs = []
        for s in range(seq_size):
            for h in range(head_size):
                g, p, c = s // (fold * share), (s // share) % fold, s % share
                other = (p * head_size + h) ^ k
                t = (g * fold + other // head_size) * share + c
                pairs.append((s * head_size + h, t * head_size + other % head_size))
        return lax.ppermute(array, ("seq", "head"), pairs)

    def seq_flip(array, bit):
        return lax.ppermute(array, "seq", [(s, s ^ bit) for s in range(seq_size)])

    sent = pl.pallas_call(
        project,
        out_shape=[jax.ShapeDtypeStruct((rows + half, LANES), bf16)] * H,
        in_specs=[SMEM, HBM, HBM],
        out_specs=[VMEM] * H,
        scratch_shapes=[
            pltpu.VMEM((rows, width), bf16),
            pltpu.VMEM((3, width, H * DH), bf16),
            pltpu.VMEM((H, rows + half, LANES), bf16),
            pltpu.SemaphoreType.DMA((7,)),
        ],
        compiler_params=pltpu.CompilerParams(vmem_limit_bytes=53 << 20),
        name="project",
    )(me_array, tokens, w_proj)
    def gating_of(tokens):
        return pl.pallas_call(
            project_gating,
            out_shape=jax.ShapeDtypeStruct((rows, H * DH), bf16),
            in_specs=[HBM, HBM],
            out_specs=VMEM,
            scratch_shapes=[
                pltpu.VMEM((rows, width), bf16),
                pltpu.VMEM((width, H * DH), bf16),
                pltpu.SemaphoreType.DMA((2,)),
            ],
            compiler_params=pltpu.CompilerParams(vmem_limit_bytes=12 << 20),
            name="project_gating",
        )(tokens, w_proj)

    start = jnp.sum((tile_user[None, :] < tile_user[:, None]).astype(jnp.int32), axis=1)
    length = jnp.sum((tile_user[None, :] == tile_user[:, None]).astype(f32), axis=1) * TILE
    asked = jnp.arange(H, dtype=jnp.int32) ^ me

    def blocks_of(places, in_group, in_core):
        in_seq = (in_group * fold + places // head_size) * share + in_core
        return in_seq * head_size + places % head_size

    order = [0, 1, 5, 4, 2, 3, 6, 7]
    place_of = jnp.array([order.index(k) for k in range(H)], jnp.int32)
    arrived = {0: sent[0]}
    for k in order[1:-2]:
        arrived[k] = partner(sent[k], k)
    first_lot = jnp.stack([arrived[k][:rows] for k in order[:TEAM]])
    *held_back, first_lot = lax.optimization_barrier((sent[order[-2]], sent[order[-1]], first_lot))
    for k, array in zip(order[-2:], held_back):
        arrived[k] = partner(array, k)
    queries = jnp.stack([arrived[k][rows:] for k in range(H)])
    lots = [first_lot, jnp.stack([arrived[k][:rows] for k in order[TEAM:]])]
    keys = jnp.concatenate(lots)
    first_places = jnp.arange(0, H, TEAM, dtype=jnp.int32)
    mine = blocks_of(asked, group, core)
    out_team = asked[::TEAM] // TEAM
    if groups == 2 and share == 2:
        far_keys = jnp.concatenate([seq_flip(lot, fold * share) for lot in lots])
        other_queries = seq_flip(queries, 1)
        others = blocks_of(asked, group, 1 - core)

        def tables(query_blocks, in_group):
            teams = blocks_of(first_places, in_group, core)
            return start, 1.0 / length, query_blocks, teams, place_of[asked], out_team

        near_ours = attend_call(tables(mine, group), queries, keys, f32)
        near_theirs = attend_call(tables(others, group), other_queries, keys, f32)
        gating = gating_of(lax.optimization_barrier((tokens, near_theirs))[0])
        far_keys, near_theirs, near_ours, gating = lax.optimization_barrier(
            (far_keys, near_theirs, near_ours, gating)
        )
        theirs = attend_call(
            tables(others, 1 - group), other_queries, far_keys, bf16, near_theirs
        )
        theirs = seq_flip(theirs, 1)
        ours = attend_call(tables(mine, 1 - group), queries, far_keys, f32, near_ours)
        attention = (ours + theirs.astype(f32)).astype(bf16)
    else:
        everything = lax.all_gather(keys, "seq", axis=0, tiled=True)
        index = jnp.arange(blocks, dtype=jnp.int32)
        slot = index // head_size * H + place_of[jnp.bitwise_xor(index % head_size, me)]
        tables = (start, 1.0 / length, mine, index[::TEAM], slot, out_team)
        attention = attend_call(tables, queries, everything, bf16)
        gating = gating_of(tokens)
    teams = [
        [
            ((g * fold + p) * share + c) * head_size + h
            for p in range(fold)
            for h in range(head_size)
        ]
        for g in range(groups)
        for c in range(share)
    ]
    returned = lax.all_to_all(
        attention, ("seq", "head"), 0, 0, axis_index_groups=teams, tiled=True
    )
    return pl.pallas_call(
        finish,
        out_shape=jax.ShapeDtypeStruct((rows, width), bf16),
        in_specs=[VMEM, VMEM, VMEM, VMEM],
        out_specs=VMEM,
        compiler_params=pltpu.CompilerParams(vmem_limit_bytes=12 << 20),
        name="finish",
    )(tokens, returned, gating, w_out)


def solution(mesh):
    placed = (P(("seq", "head"), None), P(), P(), P())
    return jax.shard_map(
        functools.partial(per_device, mesh.shape["seq"], mesh.shape["head"]),
        mesh=mesh,
        in_specs=placed,
        out_specs=P(("seq", "head"), None),
        check_vma=False,
    )
```

```python
import functools

import jax
import jax.numpy as jnp
from jax import lax
from jax.experimental import pallas as pl
from jax.experimental.pallas import tpu as pltpu
from jax.sharding import PartitionSpec as P

H = 8
DH = 64
TILE = 128
LANES = 2 * DH
TEAM = H // 2

epsilon = 1e-05

f32 = jnp.float32
bf16 = jnp.bfloat16


def layer_norm(values):
    center = values - jnp.mean(values, axis=-1, keepdims=True)
    spread = jnp.mean(center * center, axis=-1, keepdims=True)
    return center * lax.rsqrt(spread + epsilon)


def silu(values):
    half = values * 0.5
    return half + half * jnp.tanh(half)


def swap_halves(values):
    return pltpu.roll(values, DH, 1)


def low_lanes(rows):
    return lax.broadcasted_iota(jnp.int32, (rows, LANES), 1) < DH


def project(me_ref, tokens_ref, weights_ref, *refs):
    outs, (tokens, weights, held, sems) = refs[:-4], refs[-4:]
    rows = tokens.shape[0]
    half = rows // 2
    copies = [[pltpu.make_async_copy(tokens_ref, tokens, sems.at[0])]]
    deep = weights.shape[1] // 2
    for i, block in enumerate((3, 1, 2)):
        pieces = []
        for j in range(2):
            inner = pl.ds(j * deep, deep)
            source = weights_ref.at[inner, pl.ds(block * H * DH, H * DH)]
            pieces.append(
                pltpu.make_async_copy(source, weights.at[i, inner], sems.at[1 + 2 * i + j])
            )
        copies.append(pieces)
    for pieces in copies:
        for copy in pieces:
            copy.start()

    def wait(number):
        for copy in copies[number]:
            copy.wait()

    wait(0)
    normed = layer_norm(tokens[...].astype(f32)).astype(bf16)
    low, half_low = low_lanes(rows), low_lanes(half)
    scale = 0.5 * DH ** (-0.5)
    wait(1)
    keys = silu(jnp.dot(normed, weights[0], preferred_element_type=f32))
    wait(2)
    values = silu(jnp.dot(normed, weights[1], preferred_element_type=f32))
    for pair in range(H // 2):
        at = slice(pair * LANES, (pair + 1) * LANES)
        key, value = keys[:, at], values[:, at]
        held[2 * pair, :rows] = jnp.where(low, key, swap_halves(value)).astype(bf16)
        held[2 * pair + 1, :rows] = jnp.where(low, swap_halves(key), value).astype(bf16)
    wait(3)
    queries = silu(jnp.dot(normed, weights[2], preferred_element_type=f32)) * scale
    for pair in range(H // 2):
        at = slice(pair * LANES, (pair + 1) * LANES)
        upper, lower = queries[:half, at], queries[half:, at]
        held[2 * pair, rows:] = jnp.where(half_low, upper, swap_halves(lower)).astype(bf16)
        held[2 * pair + 1, rows:] = jnp.where(half_low, swap_halves(upper), lower).astype(bf16)
    for k, out in enumerate(outs):
        out[...] = held[jnp.bitwise_xor(me_ref[0], k)]


def project_gating(tokens_ref, weights_ref, out_ref, tokens, weights, sems):
    copies = [
        pltpu.make_async_copy(tokens_ref, tokens, sems.at[0]),
        pltpu.make_async_copy(weights_ref.at[:, pl.ds(0, H * DH)], weights, sems.at[1]),
    ]
    for copy in copies:
        copy.start()
    for copy in copies:
        copy.wait()
    normed = layer_norm(tokens[...].astype(f32)).astype(bf16)
    gating = silu(jnp.dot(normed, weights[...], preferred_element_type=f32))
    out_ref[...] = gating.astype(bf16)


def attend(
    start_ref, inverse_ref, block_ref, team_ref, slot_ref, out_team, queries_ref, held, *refs
):
    step = pl.program_id(0)
    *before, out_ref, total, queries = refs
    rows = held.shape[1]
    half = rows // 2
    tiles = rows // TILE
    low = low_lanes(half)
    blocks = [block_ref[step * TEAM + i] for i in range(TEAM)]
    for i in range(TEAM):
        packed = queries_ref[i].astype(f32)
        queries[i * rows : i * rows + half] = jnp.where(low, packed, 0.0).astype(bf16)
        queries[i * rows + half : (i + 1) * rows] = jnp.where(
            low, swap_halves(packed), 0.0
        ).astype(bf16)
    starts = [start_ref[block * tiles + j] for block in blocks for j in range(tiles)]
    least, low_start, high_start, high_first = blocks[0], starts[0], starts[0], starts[0]
    for block in blocks[1:]:
        least = jnp.minimum(least, block)
    for start in starts[1:]:
        low_start = jnp.minimum(low_start, start)
        high_start = jnp.maximum(high_start, start)
    for start in starts[tiles::tiles]:
        high_first = jnp.maximum(high_first, start)
    total[...] = jnp.zeros_like(total)

    def add(team, key_block, masked, chosen):
        key_rows = jnp.concatenate([held[slot_ref[team * TEAM + i]] for i in range(TEAM)], axis=0)
        if masked:
            column = lax.broadcasted_iota(jnp.int32, (TILE, TEAM * rows), 1)
            ahead = column - lax.broadcasted_iota(jnp.int32, (TILE, TEAM * rows), 0)

        def add_to(i, count=1):
            at = slice(i * rows, (i + count) * rows)
            score = lax.dot_general(
                queries[at], key_rows, (((1,), (1,)), ((), ())), preferred_element_type=f32
            )
            weights = score + score * jnp.tanh(score)
            if masked:
                pieces = []
                for j in range(tiles):
                    from_start = starts[i * tiles + j] * TILE - key_block * rows
                    to_row = (blocks[i] - key_block) * rows + j * TILE
                    allowed = (column >= from_start) & (ahead <= to_row)
                    pieces.append(jnp.where(allowed, weights[j * TILE : (j + 1) * TILE], 0.0))
                weights = jnp.concatenate(pieces, axis=0)
            total[at] += jnp.dot(weights.astype(bf16), key_rows, preferred_element_type=f32)

        if not masked:
            for i in range(0, TEAM, 2):
                add_to(i, 2)
            return
        for i in range(TEAM):
            if chosen:
                needed = starts[i * tiles] < (key_block + TEAM) * tiles
                pl.when(needed)(functools.partial(add_to, i))
            else:
                add_to(i)

    def add_diagonal(team):
        key_rows = jnp.concatenate([held[slot_ref[team * TEAM + i]] for i in range(TEAM)], axis=0)
        turn = blocks[0] - least
        for i in range(TEAM):
            seen = (i + 1) * rows
            at = pl.ds(pl.multiple_of(jnp.bitwise_xor(turn, i) * rows, rows), rows)
            score = lax.dot_general(
                queries[at], key_rows[:seen], (((1,), (1,)), ((), ())), preferred_element_type=f32
            )
            weights = score + score * jnp.tanh(score)
            column = lax.broadcasted_iota(jnp.int32, (TILE, seen), 1)
            ahead = column - lax.broadcasted_iota(jnp.int32, (TILE, seen), 0)
            pieces = []
            for j in range(tiles):
                from_start = start_ref[(least + i) * tiles + j] * TILE - least * rows
                allowed = (column >= from_start) & (ahead <= i * rows + j * TILE)
                pieces.append(jnp.where(allowed, weights[j * TILE : (j + 1) * TILE], 0.0))
            weights = jnp.concatenate(pieces, axis=0).astype(bf16)
            total[at] += jnp.dot(weights, key_rows[:seen], preferred_element_type=f32)

    def one_team(team, carry):
        key_block = team_ref[team]
        earlier = (key_block < least) & ((key_block + TEAM) * tiles > low_start)
        whole = key_block * tiles >= high_start
        every = (key_block + TEAM) * tiles > high_first
        pl.when(earlier & whole)(lambda: add(team, key_block, False, False))
        pl.when(earlier & ~every)(lambda: add(team, key_block, True, True))
        pl.when(earlier & ~whole & every)(lambda: add(team, key_block, True, False))
        pl.when(key_block == least)(lambda: add_diagonal(team))
        return carry

    lax.fori_loop(0, held.shape[0] // TEAM, one_team, 0)
    for i in range(TEAM):
        at = i * rows
        upper = total[at : at + half] * inverse_ref[blocks[i] * tiles]
        lower = total[at + half : at + rows] * inverse_ref[blocks[i] * tiles + tiles - 1]
        packed = jnp.where(low, swap_halves(upper), lower)
        for more in before:
            packed = packed + more[blocks[i] - least].astype(f32)
        out_ref[blocks[i] - least] = packed.astype(out_ref.dtype)


def attend_call(tables, queries, keys, gives, *before):
    half, rows = queries.shape[1], 2 * queries.shape[1]
    steps = queries.shape[0] // TEAM
    packed = pl.BlockSpec((TEAM, half, LANES), lambda i, *_: (i, 0, 0))
    placed = pl.BlockSpec((TEAM, half, LANES), lambda i, *refs: (refs[5][i], 0, 0))
    return pl.pallas_call(
        attend,
        grid_spec=pltpu.PrefetchScalarGridSpec(
            num_scalar_prefetch=6,
            grid=(steps,),
            in_specs=[
                packed,
                pl.BlockSpec(keys.shape, lambda i, *_: (0, 0, 0), pipeline_mode=pl.Buffered(1)),
            ]
            + [placed] * len(before),
            out_specs=placed,
            scratch_shapes=[
                pltpu.VMEM((TEAM * rows, LANES), f32),
                pltpu.VMEM((TEAM * rows, LANES), bf16),
            ],
        ),
        out_shape=jax.ShapeDtypeStruct(queries.shape, gives),
        compiler_params=pltpu.CompilerParams(vmem_limit_bytes=24 << 20),
        cost_estimate=pl.CostEstimate(
            flops=steps * 2_000_000_000, bytes_accessed=4_000_000, transcendentals=4_000_000
        ),
        name="attend",
    )(*tables, queries, keys, *before)


def finish(tokens_ref, attention_ref, gating_ref, weights_ref, out_ref):
    rows = tokens_ref.shape[0]
    half = rows // 2
    low = low_lanes(half)
    uppers, lowers = [], []
    for pair in range(H // 2):
        one = attention_ref[2 * pair].astype(f32)
        two = attention_ref[2 * pair + 1].astype(f32)
        uppers.append(jnp.where(low, one, swap_halves(two)))
        lowers.append(jnp.where(low, swap_halves(one), two))
    attention = jnp.concatenate(
        [jnp.concatenate(uppers, axis=1), jnp.concatenate(lowers, axis=1)], axis=0
    )
    gated = (layer_norm(attention) * gating_ref[...].astype(f32)).astype(bf16)
    mixed = tokens_ref[...].astype(f32) + jnp.dot(
        gated, weights_ref[...], preferred_element_type=f32
    )
    out_ref[...] = mixed.astype(bf16)


VMEM = pl.BlockSpec(memory_space=pltpu.VMEM)
SMEM = pl.BlockSpec(memory_space=pltpu.SMEM)
HBM = pl.BlockSpec(memory_space=pltpu.HBM)


def per_device(seq_size, head_size, tokens, w_proj, w_out, tile_user):
    rows, width = tokens.shape
    half = rows // 2
    tiles = rows // TILE
    blocks = seq_size * head_size
    seq, head = lax.axis_index("seq"), lax.axis_index("head")
    fold = H // head_size
    share = fold
    groups = seq_size // (fold * share)
    group, part, core = seq // (fold * share), (seq // share) % fold, seq % share
    me = part * head_size + head
    me_array = me.reshape(1).astype(jnp.int32)

    def partner(array, k):
        if k == 0:
            return array
        pairs = []
        for s in range(seq_size):
            for h in range(head_size):
                g, p, c = s // (fold * share), (s // share) % fold, s % share
                other = (p * head_size + h) ^ k
                t = (g * fold + other // head_size) * share + c
                pairs.append((s * head_size + h, t * head_size + other % head_size))
        return lax.ppermute(array, ("seq", "head"), pairs)

    def seq_flip(array, bit):
        return lax.ppermute(array, "seq", [(s, s ^ bit) for s in range(seq_size)])

    sent = pl.pallas_call(
        project,
        out_shape=[jax.ShapeDtypeStruct((rows + half, LANES), bf16)] * H,
        in_specs=[SMEM, HBM, HBM],
        out_specs=[VMEM] * H,
        scratch_shapes=[
            pltpu.VMEM((rows, width), bf16),
            pltpu.VMEM((3, width, H * DH), bf16),
            pltpu.VMEM((H, rows + half, LANES), bf16),
            pltpu.SemaphoreType.DMA((7,)),
        ],
        compiler_params=pltpu.CompilerParams(vmem_limit_bytes=53 << 20),
        name="project",
    )(me_array, tokens, w_proj)
    def gating_of(tokens):
        return pl.pallas_call(
            project_gating,
            out_shape=jax.ShapeDtypeStruct((rows, H * DH), bf16),
            in_specs=[HBM, HBM],
            out_specs=VMEM,
            scratch_shapes=[
                pltpu.VMEM((rows, width), bf16),
                pltpu.VMEM((width, H * DH), bf16),
                pltpu.SemaphoreType.DMA((2,)),
            ],
            compiler_params=pltpu.CompilerParams(vmem_limit_bytes=12 << 20),
            name="project_gating",
        )(tokens, w_proj)

    start = jnp.sum((tile_user[None, :] < tile_user[:, None]).astype(jnp.int32), axis=1)
    length = jnp.sum((tile_user[None, :] == tile_user[:, None]).astype(f32), axis=1) * TILE
    asked = jnp.arange(H, dtype=jnp.int32) ^ me

    def blocks_of(places, in_group, in_core):
        in_seq = (in_group * fold + places // head_size) * share + in_core
        return in_seq * head_size + places % head_size

    order = [0, 1, 5, 4, 2, 3, 6, 7]
    place_of = jnp.array([order.index(k) for k in range(H)], jnp.int32)
    arrived = {0: sent[0]}
    for k in order[1:-2]:
        arrived[k] = partner(sent[k], k)
    first_lot = jnp.stack([arrived[k][:rows] for k in order[:TEAM]])
    *held_back, first_lot = lax.optimization_barrier((sent[order[-2]], sent[order[-1]], first_lot))
    for k, array in zip(order[-2:], held_back):
        arrived[k] = partner(array, k)
    queries = jnp.stack([arrived[k][rows:] for k in range(H)])
    lots = [first_lot, jnp.stack([arrived[k][:rows] for k in order[TEAM:]])]
    keys = jnp.concatenate(lots)
    first_places = jnp.arange(0, H, TEAM, dtype=jnp.int32)
    mine = blocks_of(asked, group, core)
    out_team = asked[::TEAM] // TEAM
    if groups == 2 and share == 2:
        far_keys = jnp.concatenate([seq_flip(lot, fold * share) for lot in lots])
        other_queries = seq_flip(queries, 1)
        others = blocks_of(asked, group, 1 - core)

        def tables(query_blocks, in_group):
            teams = blocks_of(first_places, in_group, core)
            return start, 1.0 / length, query_blocks, teams, place_of[asked], out_team

        near_ours = attend_call(tables(mine, group), queries, keys, f32)
        near_theirs = attend_call(tables(others, group), other_queries, keys, f32)
        gating = gating_of(lax.optimization_barrier((tokens, near_theirs))[0])
        far_keys, near_theirs, near_ours, gating = lax.optimization_barrier(
            (far_keys, near_theirs, near_ours, gating)
        )
        theirs = attend_call(
            tables(others, 1 - group), other_queries, far_keys, bf16, near_theirs
        )
        theirs = seq_flip(theirs, 1)
        ours = attend_call(tables(mine, 1 - group), queries, far_keys, f32, near_ours)
        attention = (ours + theirs.astype(f32)).astype(bf16)
    else:
        everything = lax.all_gather(keys, "seq", axis=0, tiled=True)
        index = jnp.arange(blocks, dtype=jnp.int32)
        slot = index // head_size * H + place_of[jnp.bitwise_xor(index % head_size, me)]
        tables = (start, 1.0 / length, mine, index[::TEAM], slot, out_team)
        attention = attend_call(tables, queries, everything, bf16)
        gating = gating_of(tokens)
    teams = [
        [
            ((g * fold + p) * share + c) * head_size + h
            for p in range(fold)
            for h in range(head_size)
        ]
        for g in range(groups)
        for c in range(share)
    ]
    returned = lax.all_to_all(
        attention, ("seq", "head"), 0, 0, axis_index_groups=teams, tiled=True
    )
    return pl.pallas_call(
        finish,
        out_shape=jax.ShapeDtypeStruct((rows, width), bf16),
        in_specs=[VMEM, VMEM, VMEM, VMEM],
        out_specs=VMEM,
        compiler_params=pltpu.CompilerParams(vmem_limit_bytes=12 << 20),
        name="finish",
    )(tokens, returned, gating, w_out)


def solution(mesh):
    placed = (P(("seq", "head"), None), P(), P(), P())
    return jax.shard_map(
        functools.partial(per_device, mesh.shape["seq"], mesh.shape["head"]),
        mesh=mesh,
        in_specs=placed,
        out_specs=P(("seq", "head"), None),
        check_vma=False,
    )
```

```python
import functools

import jax
import jax.numpy as jnp
from jax import lax
from jax.experimental import pallas as pl
from jax.experimental.pallas import tpu as pltpu
from jax.sharding import PartitionSpec as P

H = 8
DH = 64
TILE = 128
LANES = 2 * DH
TEAM = H // 2

epsilon = 1e-05

f32 = jnp.float32
bf16 = jnp.bfloat16


def layer_norm(values):
    center = values - jnp.mean(values, axis=-1, keepdims=True)
    spread = jnp.mean(center * center, axis=-1, keepdims=True)
    return center * lax.rsqrt(spread + epsilon)


def silu(values):
    half = values * 0.5
    return half + half * jnp.tanh(half)


def swap_halves(values):
    return pltpu.roll(values, DH, 1)


def low_lanes(rows):
    return lax.broadcasted_iota(jnp.int32, (rows, LANES), 1) < DH


def project(me_ref, tokens_ref, weights_ref, *refs):
    outs, (tokens, weights, held, sems) = refs[:-4], refs[-4:]
    rows = tokens.shape[0]
    half = rows // 2
    copies = [[pltpu.make_async_copy(tokens_ref, tokens, sems.at[0])]]
    deep = weights.shape[1] // 2
    for i, block in enumerate((3, 1, 2)):
        pieces = []
        for j in range(2):
            inner = pl.ds(j * deep, deep)
            source = weights_ref.at[inner, pl.ds(block * H * DH, H * DH)]
            pieces.append(
                pltpu.make_async_copy(source, weights.at[i, inner], sems.at[1 + 2 * i + j])
            )
        copies.append(pieces)
    for pieces in copies:
        for copy in pieces:
            copy.start()

    def wait(number):
        for copy in copies[number]:
            copy.wait()

    wait(0)
    normed = layer_norm(tokens[...].astype(f32)).astype(bf16)
    low, half_low = low_lanes(rows), low_lanes(half)
    scale = 0.5 * DH ** (-0.5)
    wait(1)
    keys = silu(jnp.dot(normed, weights[0], preferred_element_type=f32))
    wait(2)
    values = silu(jnp.dot(normed, weights[1], preferred_element_type=f32))
    for pair in range(H // 2):
        at = slice(pair * LANES, (pair + 1) * LANES)
        key, value = keys[:, at], values[:, at]
        held[2 * pair, :rows] = jnp.where(low, key, swap_halves(value)).astype(bf16)
        held[2 * pair + 1, :rows] = jnp.where(low, swap_halves(key), value).astype(bf16)
    wait(3)
    queries = silu(jnp.dot(normed, weights[2], preferred_element_type=f32)) * scale
    for pair in range(H // 2):
        at = slice(pair * LANES, (pair + 1) * LANES)
        upper, lower = queries[:half, at], queries[half:, at]
        held[2 * pair, rows:] = jnp.where(half_low, upper, swap_halves(lower)).astype(bf16)
        held[2 * pair + 1, rows:] = jnp.where(half_low, swap_halves(upper), lower).astype(bf16)
    for k, out in enumerate(outs):
        out[...] = held[jnp.bitwise_xor(me_ref[0], k)]


def project_gating(tokens_ref, weights_ref, out_ref, tokens, weights, sems):
    copies = [
        pltpu.make_async_copy(tokens_ref, tokens, sems.at[0]),
        pltpu.make_async_copy(weights_ref.at[:, pl.ds(0, H * DH)], weights, sems.at[1]),
    ]
    for copy in copies:
        copy.start()
    for copy in copies:
        copy.wait()
    normed = layer_norm(tokens[...].astype(f32)).astype(bf16)
    gating = silu(jnp.dot(normed, weights[...], preferred_element_type=f32))
    out_ref[...] = gating.astype(bf16)


def attend(
    start_ref, inverse_ref, block_ref, team_ref, slot_ref, out_team, queries_ref, held, *refs
):
    step = pl.program_id(0)
    *before, out_ref, total, queries = refs
    rows = held.shape[1]
    half = rows // 2
    tiles = rows // TILE
    low = low_lanes(half)
    blocks = [block_ref[step * TEAM + i] for i in range(TEAM)]
    for i in range(TEAM):
        packed = queries_ref[i].astype(f32)
        queries[i * rows : i * rows + half] = jnp.where(low, packed, 0.0).astype(bf16)
        queries[i * rows + half : (i + 1) * rows] = jnp.where(
            low, swap_halves(packed), 0.0
        ).astype(bf16)
    starts = [start_ref[block * tiles + j] for block in blocks for j in range(tiles)]
    least, low_start, high_start, high_first = blocks[0], starts[0], starts[0], starts[0]
    for block in blocks[1:]:
        least = jnp.minimum(least, block)
    for start in starts[1:]:
        low_start = jnp.minimum(low_start, start)
        high_start = jnp.maximum(high_start, start)
    for start in starts[tiles::tiles]:
        high_first = jnp.maximum(high_first, start)
    total[...] = jnp.zeros_like(total)

    def add(team, key_block, masked, chosen):
        key_rows = jnp.concatenate([held[slot_ref[team * TEAM + i]] for i in range(TEAM)], axis=0)
        if masked:
            column = lax.broadcasted_iota(jnp.int32, (TILE, TEAM * rows), 1)
            ahead = column - lax.broadcasted_iota(jnp.int32, (TILE, TEAM * rows), 0)

        def add_to(i, count=1):
            at = slice(i * rows, (i + count) * rows)
            score = lax.dot_general(
                queries[at], key_rows, (((1,), (1,)), ((), ())), preferred_element_type=f32
            )
            weights = score + score * jnp.tanh(score)
            if masked:
                pieces = []
                for j in range(tiles):
                    from_start = starts[i * tiles + j] * TILE - key_block * rows
                    to_row = (blocks[i] - key_block) * rows + j * TILE
                    allowed = (column >= from_start) & (ahead <= to_row)
                    pieces.append(jnp.where(allowed, weights[j * TILE : (j + 1) * TILE], 0.0))
                weights = jnp.concatenate(pieces, axis=0)
            total[at] += jnp.dot(weights.astype(bf16), key_rows, preferred_element_type=f32)

        if not masked:
            for i in range(0, TEAM, 2):
                add_to(i, 2)
            return
        for i in range(TEAM):
            if chosen:
                needed = starts[i * tiles] < (key_block + TEAM) * tiles
                pl.when(needed)(functools.partial(add_to, i))
            else:
                add_to(i)

    def add_diagonal(team):
        key_rows = jnp.concatenate([held[slot_ref[team * TEAM + i]] for i in range(TEAM)], axis=0)
        turn = blocks[0] - least
        for i in range(TEAM):
            seen = (i + 1) * rows
            at = pl.ds(pl.multiple_of(jnp.bitwise_xor(turn, i) * rows, rows), rows)
            score = lax.dot_general(
                queries[at], key_rows[:seen], (((1,), (1,)), ((), ())), preferred_element_type=f32
            )
            weights = score + score * jnp.tanh(score)
            column = lax.broadcasted_iota(jnp.int32, (TILE, seen), 1)
            ahead = column - lax.broadcasted_iota(jnp.int32, (TILE, seen), 0)
            pieces = []
            for j in range(tiles):
                from_start = start_ref[(least + i) * tiles + j] * TILE - least * rows
                allowed = (column >= from_start) & (ahead <= i * rows + j * TILE)
                pieces.append(jnp.where(allowed, weights[j * TILE : (j + 1) * TILE], 0.0))
            weights = jnp.concatenate(pieces, axis=0).astype(bf16)
            total[at] += jnp.dot(weights, key_rows[:seen], preferred_element_type=f32)

    def one_team(team, carry):
        key_block = team_ref[team]
        earlier = (key_block < least) & ((key_block + TEAM) * tiles > low_start)
        whole = key_block * tiles >= high_start
        every = (key_block + TEAM) * tiles > high_first
        pl.when(earlier & whole)(lambda: add(team, key_block, False, False))
        pl.when(earlier & ~every)(lambda: add(team, key_block, True, True))
        pl.when(earlier & ~whole & every)(lambda: add(team, key_block, True, False))
        pl.when(key_block == least)(lambda: add_diagonal(team))
        return carry

    lax.fori_loop(0, held.shape[0] // TEAM, one_team, 0)
    for i in range(TEAM):
        at = i * rows
        upper = total[at : at + half] * inverse_ref[blocks[i] * tiles]
        lower = total[at + half : at + rows] * inverse_ref[blocks[i] * tiles + tiles - 1]
        packed = jnp.where(low, swap_halves(upper), lower)
        for more in before:
            packed = packed + more[blocks[i] - least].astype(f32)
        out_ref[blocks[i] - least] = packed.astype(out_ref.dtype)


def attend_call(tables, queries, keys, gives, *before):
    half, rows = queries.shape[1], 2 * queries.shape[1]
    steps = queries.shape[0] // TEAM
    packed = pl.BlockSpec((TEAM, half, LANES), lambda i, *_: (i, 0, 0))
    placed = pl.BlockSpec((TEAM, half, LANES), lambda i, *refs: (refs[5][i], 0, 0))
    return pl.pallas_call(
        attend,
        grid_spec=pltpu.PrefetchScalarGridSpec(
            num_scalar_prefetch=6,
            grid=(steps,),
            in_specs=[
                packed,
                pl.BlockSpec(keys.shape, lambda i, *_: (0, 0, 0), pipeline_mode=pl.Buffered(1)),
            ]
            + [placed] * len(before),
            out_specs=placed,
            scratch_shapes=[
                pltpu.VMEM((TEAM * rows, LANES), f32),
                pltpu.VMEM((TEAM * rows, LANES), bf16),
            ],
        ),
        out_shape=jax.ShapeDtypeStruct(queries.shape, gives),
        compiler_params=pltpu.CompilerParams(vmem_limit_bytes=24 << 20),
        cost_estimate=pl.CostEstimate(
            flops=steps * 2_000_000_000, bytes_accessed=4_000_000, transcendentals=4_000_000
        ),
        name="attend",
    )(*tables, queries, keys, *before)


def finish(tokens_ref, attention_ref, gating_ref, weights_ref, out_ref):
    rows = tokens_ref.shape[0]
    half = rows // 2
    low = low_lanes(half)
    uppers, lowers = [], []
    for pair in range(H // 2):
        one = attention_ref[2 * pair].astype(f32)
        two = attention_ref[2 * pair + 1].astype(f32)
        uppers.append(jnp.where(low, one, swap_halves(two)))
        lowers.append(jnp.where(low, swap_halves(one), two))
    attention = jnp.concatenate(
        [jnp.concatenate(uppers, axis=1), jnp.concatenate(lowers, axis=1)], axis=0
    )
    gated = (layer_norm(attention) * gating_ref[...].astype(f32)).astype(bf16)
    mixed = tokens_ref[...].astype(f32) + jnp.dot(
        gated, weights_ref[...], preferred_element_type=f32
    )
    out_ref[...] = mixed.astype(bf16)


VMEM = pl.BlockSpec(memory_space=pltpu.VMEM)
SMEM = pl.BlockSpec(memory_space=pltpu.SMEM)
HBM = pl.BlockSpec(memory_space=pltpu.HBM)


def per_device(seq_size, head_size, tokens, w_proj, w_out, tile_user):
    rows, width = tokens.shape
    half = rows // 2
    tiles = rows // TILE
    blocks = seq_size * head_size
    seq, head = lax.axis_index("seq"), lax.axis_index("head")
    fold = H // head_size
    share = fold
    groups = seq_size // (fold * share)
    group, part, core = seq // (fold * share), (seq // share) % fold, seq % share
    me = part * head_size + head
    me_array = me.reshape(1).astype(jnp.int32)

    def partner(array, k):
        if k == 0:
            return array
        pairs = []
        for s in range(seq_size):
            for h in range(head_size):
                g, p, c = s // (fold * share), (s // share) % fold, s % share
                other = (p * head_size + h) ^ k
                t = (g * fold + other // head_size) * share + c
                pairs.append((s * head_size + h, t * head_size + other % head_size))
        return lax.ppermute(array, ("seq", "head"), pairs)

    def seq_flip(array, bit):
        return lax.ppermute(array, "seq", [(s, s ^ bit) for s in range(seq_size)])

    sent = pl.pallas_call(
        project,
        out_shape=[jax.ShapeDtypeStruct((rows + half, LANES), bf16)] * H,
        in_specs=[SMEM, HBM, HBM],
        out_specs=[VMEM] * H,
        scratch_shapes=[
            pltpu.VMEM((rows, width), bf16),
            pltpu.VMEM((3, width, H * DH), bf16),
            pltpu.VMEM((H, rows + half, LANES), bf16),
            pltpu.SemaphoreType.DMA((7,)),
        ],
        compiler_params=pltpu.CompilerParams(vmem_limit_bytes=53 << 20),
        name="project",
    )(me_array, tokens, w_proj)
    def gating_of(tokens):
        return pl.pallas_call(
            project_gating,
            out_shape=jax.ShapeDtypeStruct((rows, H * DH), bf16),
            in_specs=[HBM, HBM],
            out_specs=VMEM,
            scratch_shapes=[
                pltpu.VMEM((rows, width), bf16),
                pltpu.VMEM((width, H * DH), bf16),
                pltpu.SemaphoreType.DMA((2,)),
            ],
            compiler_params=pltpu.CompilerParams(vmem_limit_bytes=12 << 20),
            name="project_gating",
        )(tokens, w_proj)

    start = jnp.sum((tile_user[None, :] < tile_user[:, None]).astype(jnp.int32), axis=1)
    length = jnp.sum((tile_user[None, :] == tile_user[:, None]).astype(f32), axis=1) * TILE
    asked = jnp.arange(H, dtype=jnp.int32) ^ me

    def blocks_of(places, in_group, in_core):
        in_seq = (in_group * fold + places // head_size) * share + in_core
        return in_seq * head_size + places % head_size

    order = [0, 1, 5, 4, 2, 3, 6, 7]
    place_of = jnp.array([order.index(k) for k in range(H)], jnp.int32)
    arrived = {0: sent[0]}
    for k in order[1:-2]:
        arrived[k] = partner(sent[k], k)
    first_lot = jnp.stack([arrived[k][:rows] for k in order[:TEAM]])
    *held_back, first_lot = lax.optimization_barrier((sent[order[-2]], sent[order[-1]], first_lot))
    for k, array in zip(order[-2:], held_back):
        arrived[k] = partner(array, k)
    queries = jnp.stack([arrived[k][rows:] for k in range(H)])
    lots = [first_lot, jnp.stack([arrived[k][:rows] for k in order[TEAM:]])]
    keys = jnp.concatenate(lots)
    first_places = jnp.arange(0, H, TEAM, dtype=jnp.int32)
    mine = blocks_of(asked, group, core)
    out_team = asked[::TEAM] // TEAM
    if groups == 2 and share == 2:
        far_keys = jnp.concatenate([seq_flip(lot, fold * share) for lot in lots])
        other_queries = seq_flip(queries, 1)
        others = blocks_of(asked, group, 1 - core)

        def tables(query_blocks, in_group):
            teams = blocks_of(first_places, in_group, core)
            return start, 1.0 / length, query_blocks, teams, place_of[asked], out_team

        near_ours = attend_call(tables(mine, group), queries, keys, f32)
        near_theirs = attend_call(tables(others, group), other_queries, keys, f32)
        gating = gating_of(lax.optimization_barrier((tokens, near_theirs))[0])
        far_keys, near_theirs, near_ours, gating = lax.optimization_barrier(
            (far_keys, near_theirs, near_ours, gating)
        )

        def add_far(queries, query_blocks, sums, gives):
            return lax.cond(
                group > 0,
                lambda: attend_call(
                    tables(query_blocks, 1 - group), queries, far_keys, gives, sums
                ),
                lambda: sums.astype(gives),
            )

        theirs = seq_flip(add_far(other_queries, others, near_theirs, bf16), 1)
        ours = add_far(queries, mine, near_ours, f32)
        attention = (ours + theirs.astype(f32)).astype(bf16)
    else:
        everything = lax.all_gather(keys, "seq", axis=0, tiled=True)
        index = jnp.arange(blocks, dtype=jnp.int32)
        slot = index // head_size * H + place_of[jnp.bitwise_xor(index % head_size, me)]
        tables = (start, 1.0 / length, mine, index[::TEAM], slot, out_team)
        attention = attend_call(tables, queries, everything, bf16)
        gating = gating_of(tokens)
    teams = [
        [
            ((g * fold + p) * share + c) * head_size + h
            for p in range(fold)
            for h in range(head_size)
        ]
        for g in range(groups)
        for c in range(share)
    ]
    returned = lax.all_to_all(
        attention, ("seq", "head"), 0, 0, axis_index_groups=teams, tiled=True
    )
    return pl.pallas_call(
        finish,
        out_shape=jax.ShapeDtypeStruct((rows, width), bf16),
        in_specs=[VMEM, VMEM, VMEM, VMEM],
        out_specs=VMEM,
        compiler_params=pltpu.CompilerParams(vmem_limit_bytes=12 << 20),
        name="finish",
    )(tokens, returned, gating, w_out)


def solution(mesh):
    placed = (P(("seq", "head"), None), P(), P(), P())
    return jax.shard_map(
        functools.partial(per_device, mesh.shape["seq"], mesh.shape["head"]),
        mesh=mesh,
        in_specs=placed,
        out_specs=P(("seq", "head"), None),
        check_vma=False,
    )
```
